768 devices in a mesh: node: 16 (over y, core), local: 48 (over x, z).
Axes of the slice: x: 4, y: 8, z: 12, core: 2. Of those that a mesh axis runs over, the one named last changes fastest.
Arguments:
- cotangent: float32 [6144, 3584], P('local', 'node'), may hold values from -6 to 6
- probs: float32 [6144, 8], P('local'), may hold values from 0.1 to 0.8
- routes: int32 [6144, 8], P('local'), may hold values from 0 to 143, all different within a row; in each aligned block of 128 rows (0 to 127, 128 to 255, ...) at most 9 rows name the same one
- gate_pre: bfloat16 [144, 432, 1024], P('local'), may hold values from -3 to 3
- up_pre: bfloat16 [144, 432, 1024], P('local'), may hold values from -3 to 3
- w_gate: bfloat16 [144, 3584, 1024], P('local', 'node'), may hold values from -0.1875 to 0.1875
- w_up: bfloat16 [144, 3584, 1024], P('local', 'node'), may hold values from -0.1875 to 0.1875
- w_down: bfloat16 [144, 3584, 1024], P('local', 'node'), may hold values from -0.1875 to 0.1875
Outputs:
- grad_tokens: float32 [6144, 3584], P('local', 'node')
- grad_probs: float32 [6144, 8], P('local')
The draws below stay inside these ranges and needn't reach their ends.
Inputs may be any that keep to these rules, and one draw needn't show every extreme that they name: `routes`: each row names 8 different experts; in each aligned block of 128 rows (the tokens of one local shard) no expert is named more than 9 times, a bound that some block reaches.
All inputs are finite; a program needn't handle non-finite values.
Results may differ from the reference program's by a relative error of at most 0.0049.
Values may be sent and summed in bfloat16 or wider, within the bound.
No kernel may reach another device: no remote copies, remote signals or barrier semaphores. Data moves between devices by JAX's collectives and lax.ppermute only.
A program may use at most 64 MiB of HBM per device.

```python
import math
import jax
import jax.numpy as jnp
import numpy as np
from jax import lax

D = 3584
HID = 1024
EXPERTS = 144
TOPK = 8
TOK_LOCAL = 128
MOST = 9
CAP = 432
TOKENS = 6144
N_LOCAL = 48


def block_levels(rng, extent, shards, low, largest):
    gain, own = 1.0, jax.random.fold_in(rng, 6)
    for axis_at, parts in shards:
        steps = jnp.exp(jax.random.uniform(jax.random.fold_in(own, axis_at), (parts,), jnp.float32, low / len(shards), largest / len(shards)))
        gain = gain * jnp.repeat(steps, extent[axis_at] // parts).reshape([-1 if axis == axis_at else 1 for axis in range(len(extent))])
    return gain


def shared_out(own_key, own, number, rows, amount, top, limit, skew):
    order = jax.random.permutation(own_key, amount)
    crowded, usual = load_shares(amount, rows * top, limit, skew, True), load_shares(amount, rows * top, limit, skew, False)
    places = jnp.arange(amount)

    def named(lengths, turn):
        used = int((lengths > 0).sum())
        fixed = max(1, used // 4)
        passed = fixed + (places - fixed + turn * (used - fixed)) % max(1, amount - fixed)
        return jnp.zeros((amount,), jnp.int32).at[order[jnp.where(places < fixed, places, passed)]].set(jnp.asarray(lengths, jnp.int32))

    lengths = jnp.where(number % 4 == 0, named(crowded, number // 4), named(usual, number - number // 4 - 1))
    mixed = jax.random.permutation(jax.random.fold_in(own, 3), amount)
    giver, sink = mixed[0:amount // 2 * 2:2], mixed[1:amount // 2 * 2:2]
    slack = jnp.minimum(lengths[giver] - 1, limit - lengths[sink]) // 2
    slack = jnp.where((giver == order[0]) | (sink == order[0]) | (lengths[sink] == 0), 0, jnp.maximum(slack, 0))
    passed = jax.random.randint(jax.random.fold_in(own, 4), (amount // 2,), 0, 1 << 20) % (slack + 1)
    lengths = lengths.at[giver].add(-passed).at[sink].add(passed)
    items = jnp.searchsorted(jnp.cumsum(lengths), jnp.arange(rows * top), side="right").astype(jnp.int32)
    listing = items.reshape(top, rows).T
    listing = listing[jax.random.permutation(jax.random.fold_in(own, 1), rows)]
    turn = jax.random.randint(jax.random.fold_in(own, 2), (rows, 1), 0, top)
    return jnp.take_along_axis(listing, (jnp.arange(top)[None, :] + turn) % top, axis=1)


def load_shares(amount, total, limit, skew, full):
    portions = [(1 << 20) // math.isqrt(rank ** skew) + 1 for rank in range(1, amount + 1)]
    largest = limit if full else min(limit, max(-(-total // amount), total * portions[0] // sum(portions)))
    least = 1 if total - largest >= amount - 1 else 0
    holding, surplus = [largest] + [least] * (amount - 1), total - largest - least * (amount - 1)
    while surplus > 0:
        movable = [i for i in range(1, amount) if holding[i] < largest] or [i for i in range(1, amount) if holding[i] < limit]
        mass, remaining = sum([portions[i] for i in movable]), surplus
        for i in movable:
            addition = min(limit - holding[i], max(1, remaining * portions[i] // mass), surplus)
            holding[i] = holding[i] + addition
            surplus = surplus - addition
    return np.array(holding)


def scatter_about(key, shape, spread, most, shards=(), kind=jnp.bfloat16):
    factor_of = block_levels(key, shape, shards, -0.22, 0.18) if shards else 1.0
    result = jax.random.normal(key, shape, jnp.float32) * spread * factor_of
    return jnp.minimum(jnp.maximum(result, -most), most).astype(kind)


def setup_inputs(seed: int = 0) -> dict:
    splits = jax.random.split(jax.random.key(seed), 9)
    cotangent = scatter_about(splits[0], (TOKENS, D), 0.4, 6.0, ((0, 48), (1, 16)), jnp.float32)
    probs = jnp.clip(0.1 + 0.7 * jax.random.uniform(splits[1], (TOKENS, TOPK), jnp.float32) ** block_levels(splits[1], (TOKENS, TOPK), ((0, 48),), -0.2, 0.2), 0.1, 0.8)
    routes_keys = jax.random.split(jax.random.fold_in(splits[2], 1), TOKENS // TOK_LOCAL)
    routes_turns = jax.random.permutation(jax.random.fold_in(splits[2], 3), TOKENS // TOK_LOCAL)
    routes = jax.vmap(lambda own, number: shared_out(jax.random.fold_in(splits[2], 2), own, number, TOK_LOCAL, EXPERTS, TOPK, MOST, 2))(routes_keys, routes_turns).reshape((TOKENS, TOPK))
    gate_pre = scatter_about(splits[3], (EXPERTS, CAP, HID), 0.5, 3.0, ((0, 48),))
    up_pre = scatter_about(splits[4], (EXPERTS, CAP, HID), 0.5, 3.0, ((0, 48),))
    w_gate = scatter_about(splits[5], (EXPERTS, D, HID), HID ** -0.5, 0.1875, ((0, 48), (1, 16)))
    w_up = scatter_about(splits[6], (EXPERTS, D, HID), HID ** -0.5, 0.1875, ((0, 48), (1, 16)))
    w_down = scatter_about(splits[7], (EXPERTS, D, HID), HID ** -0.5, 0.1875, ((0, 48), (1, 16)))
    return dict(cotangent=cotangent, probs=probs, routes=routes, gate_pre=gate_pre, up_pre=up_pre, w_gate=w_gate, w_up=w_up, w_down=w_down)


def reference(cotangent, probs, routes, gate_pre, up_pre, w_gate, w_up, w_down):
    by_shard = routes.reshape(N_LOCAL, TOK_LOCAL * TOPK)
    experts_iota = jnp.arange(EXPERTS, dtype=jnp.int32)
    onehot = (by_shard[:, :, None] == experts_iota).astype(jnp.int32)
    before = jnp.cumsum(onehot, axis=1) - onehot
    slot_rank = jnp.sum(before * onehot, axis=2)
    shard_ids = jnp.arange(N_LOCAL, dtype=jnp.int32)[:, None]
    position = (shard_ids * MOST + slot_rank).reshape(-1).astype(jnp.int32)
    expert_ids = routes.reshape(-1).astype(jnp.int32)
    token_ids = (jnp.arange(TOKENS * TOPK, dtype=jnp.int32) // TOPK).astype(jnp.int32)
    owner = jnp.full((EXPERTS, CAP), TOKENS, jnp.int32).at[expert_ids, position].set(token_ids)
    weight_low = jnp.zeros((EXPERTS, CAP), jnp.bfloat16).at[expert_ids, position].set(probs.reshape(-1).astype(jnp.bfloat16))
    weight_low = lax.optimization_barrier(weight_low)
    cotan_low = cotangent.astype(jnp.bfloat16)
    padded = jnp.concatenate([cotan_low, jnp.zeros((1, D), jnp.bfloat16)], axis=0)

    def one_expert(accumulated, expert):
        buffer_rows = padded[owner[expert]]
        grad_hidden = jnp.dot(buffer_rows, w_down[expert], preferred_element_type=jnp.float32)
        gate_value = gate_pre[expert].astype(jnp.float32)
        up_value = up_pre[expert].astype(jnp.float32)
        sigmoid_gate = jax.nn.sigmoid(gate_value)
        silu_gate = gate_value * sigmoid_gate
        hidden_act = silu_gate * up_value
        score_rows = jnp.sum(hidden_act * grad_hidden, axis=1)
        scaled = weight_low[expert].astype(jnp.float32)[:, None] * grad_hidden
        grad_up = (scaled * silu_gate).astype(jnp.bfloat16)
        grad_gate = (scaled * up_value * sigmoid_gate * (1.0 + gate_value * (1.0 - sigmoid_gate))).astype(jnp.bfloat16)
        back_rows = jnp.dot(grad_gate, w_gate[expert].T, preferred_element_type=jnp.float32)
        back_rows = back_rows + jnp.dot(grad_up, w_up[expert].T, preferred_element_type=jnp.float32)
        accumulated = accumulated.at[owner[expert]].add(back_rows)
        return accumulated, score_rows

    totals, scores = lax.scan(one_expert, jnp.zeros((TOKENS + 1, D), jnp.float32), jnp.arange(EXPERTS, dtype=jnp.int32))
    grad_tokens = totals[:TOKENS]
    grad_probs = scores[expert_ids, position].reshape(TOKENS, TOPK)
    return grad_tokens, grad_probs
```

```python
import functools

import jax
import jax.numpy as jnp
import numpy as np
from jax import lax
from jax.experimental import pallas as pl
from jax.experimental.pallas import tpu as pltpu
from jax.sharding import Mesh, PartitionSpec as P

MOST = 9
OWN = 3
SLOTS = 28
PAIR = 2 * SLOTS
LANE = 128
GROUP = 16
F32 = jnp.float32
BF16 = jnp.bfloat16
NT = (((1,), (1,)), ((), ()))
VMEM = pl.BlockSpec(memory_space=pltpu.VMEM)
SMEM = pl.BlockSpec(memory_space=pltpu.SMEM)
PARAMS = pltpu.CompilerParams(vmem_limit_bytes=48 * 1024 * 1024)


def dot(a, b):
    return jnp.dot(a, b, preferred_element_type=F32)


def dot_nt(a, b):
    return lax.dot_general(a, b, NT, preferred_element_type=F32)


def decode(row):
    second = (row >= SLOTS).astype(jnp.int32)
    place = row - SLOTS * second
    expert = (place >= MOST).astype(jnp.int32) + (place >= 2 * MOST).astype(jnp.int32)
    expert = jnp.minimum(expert, OWN - 1)
    return second, expert, place - MOST * expert


def rank_table(routes, experts):
    tokens, top = routes.shape
    lane = lax.broadcasted_iota(jnp.int32, (tokens, experts), 1)
    hits = [routes[:, k : k + 1] == lane for k in range(top)]
    named = sum(hit.astype(F32) for hit in hits)
    square = (tokens, tokens)
    earlier = lax.broadcasted_iota(jnp.int32, square, 0) > lax.broadcasted_iota(jnp.int32, square, 1)
    rank = dot(earlier.astype(F32).astype(BF16), named.astype(BF16))
    return hits, jnp.where(named > 0.0, rank, 31.0).astype(BF16)


def expert_rows(first, homes, experts):
    shape = (homes, PAIR, experts)
    _, expert, _ = decode(lax.broadcasted_iota(jnp.int32, shape, 1))
    wanted = (lax.broadcasted_iota(jnp.int32, shape, 0) + first) * OWN + expert
    return (lax.broadcasted_iota(jnp.int32, shape, 2) == wanted).reshape(homes * PAIR, experts)


def send_kernel(homes, routes_ref, probs_ref, cot_ref, out_ref, right):
    tokens, width = cot_ref.shape
    experts = homes * OWN
    routes = routes_ref[...]
    hits, ranks = rank_table(routes, experts)
    probs = probs_ref[...]
    weight = sum(jnp.where(hit, probs[:, k : k + 1], 0.0) for k, hit in enumerate(hits)).astype(BF16)
    right[...] = jnp.zeros_like(right)
    right[0:tokens, :] = cot_ref[:, 0:LANE].astype(BF16)
    right[tokens : 2 * tokens, 0 : width - LANE] = cot_ref[:, LANE:width].astype(BF16)
    mark = lax.broadcasted_iota(jnp.int32, (tokens, LANE), 1) == width - LANE
    right[2 * tokens : 3 * tokens, :] = mark.astype(F32).astype(BF16)
    step = 8 if homes % 8 == 0 else homes
    for first in range(0, homes, step):
        pick = expert_rows(first, step, experts).astype(F32).astype(BF16)
        rank_of = dot_nt(pick, ranks)
        weight_of = dot_nt(pick, weight)
        shape = (step, PAIR, tokens)
        second, _, slot = decode(lax.broadcasted_iota(jnp.int32, shape, 1))
        second = second.reshape(step * PAIR, tokens) > 0
        here = rank_of == slot.astype(F32).reshape(step * PAIR, tokens)
        left = jnp.concatenate(
            [
                jnp.where(here & ~second, 1.0, 0.0).astype(BF16),
                jnp.where(here & second, 1.0, 0.0).astype(BF16),
                jnp.where(here & second, weight_of, 0.0).astype(BF16),
            ],
            axis=1,
        )
        out_ref[first * PAIR : (first + step) * PAIR, :] = dot(left, right[...]).astype(BF16)


def down_half(half, share, rows_ref, w_ref, out_ref):
    capacity = out_ref.shape[1] - share
    whole = half * (OWN - 1)
    width = w_ref.shape[1]
    hidden = w_ref.shape[2]
    left = rows_ref[whole, 0:capacity, 0:width]
    part = rows_ref[1, pl.ds(pl.multiple_of(half * share, 16), share), 0:width]
    tile = 2 * LANE
    for n in range(hidden // tile):
        columns = slice(n * tile, (n + 1) * tile)
        for a, top, count in (
            (dot(left, w_ref[whole, :, columns]), 0, capacity),
            (dot(part, w_ref[1, :, columns]), capacity, share),
        ):
            out_ref[2 * n, top : top + count, :] = a[:, :LANE].astype(BF16)
            out_ref[2 * n + 1, top : top + count, :] = a[:, LANE:].astype(BF16)


def unpack_kernel(share, half_ref, got_ref, w_ref, rows_ref, out_ref):
    sources = got_ref.shape[0] // PAIR
    capacity = sources * MOST
    rows, columns = GROUP * MOST, GROUP * PAIR
    at = lax.broadcasted_iota(jnp.int32, (1, columns), 1)
    source = jnp.floor((at.astype(F32) + 0.5) * (1.0 / PAIR)).astype(jnp.int32)
    second, expert, slot = decode(at - PAIR * source)
    goal = jnp.where(slot < MOST, (2 * expert + second) * rows + source * MOST + slot, -1)
    select = lax.broadcasted_iota(jnp.int32, (2 * OWN * rows, columns), 0) == goal
    select = select.astype(F32).astype(BF16)
    rows_ref[:, capacity:, :] = jnp.zeros((OWN, rows_ref.shape[1] - capacity, 2 * LANE), BF16)
    for g in range(sources // GROUP):
        piece = dot(select, got_ref[g * columns : (g + 1) * columns, :]).astype(BF16)
        for e in range(OWN):
            for second in range(2):
                top = (2 * e + second) * rows
                rows_ref[e, g * rows : (g + 1) * rows, second * LANE : (second + 1) * LANE] = piece[top : top + rows]
    down_half(1 - half_ref[0], share, rows_ref, w_ref, out_ref)


def down_kernel(share, half_ref, rows_ref, w_ref, out_ref):
    down_half(half_ref[0], share, rows_ref, w_ref, out_ref)


def back_kernel(share, grad_ref, rows_ref, gate_ref, up_ref, wg_ref, wu_ref, out_ref, gate_grad, up_grad, weight, score, back):
    sources = out_ref.shape[0] // PAIR
    capacity = sources * MOST
    width = wg_ref.shape[1]
    blocks = gate_ref.shape[2] // LANE
    rows, columns = GROUP * MOST, GROUP * PAIR
    tail = capacity - share
    for e, low, count, half, top in (
        (0, 0, capacity, 0, 0),
        (OWN - 1, 0, capacity, 1, 0),
        (1, 0, share, 0, capacity),
        (1, share, tail, 1, capacity),
    ):
        here = slice(0, count)
        weight[here] = jnp.broadcast_to(
            rows_ref[e, low : low + count, LANE:].astype(F32)[:, width - LANE : width - LANE + 1], (count, LANE)
        )
        score[here] = jnp.zeros((count, LANE), F32)

        def block(b, carry, e=e, low=low, count=count, half=half, top=top, here=here):
            columns = pl.ds(pl.multiple_of(b * LANE, LANE), LANE)
            grad = grad_ref[2 * b + half, top : top + count, :].astype(F32)
            gate = gate_ref[e, low : low + count, columns].astype(F32)
            up = up_ref[e, low : low + count, columns].astype(F32)
            sig = lax.logistic(gate)
            silu = gate * sig
            score[here] += silu * up * grad
            scaled = weight[here] * grad
            up_grad[here, columns] = (scaled * silu).astype(BF16)
            gate_grad[here, columns] = (scaled * up * sig * (1.0 + gate * (1.0 - sig))).astype(BF16)
            return carry

        lax.fori_loop(0, blocks, block, 0)
        total = dot_nt(gate_grad[here], wg_ref[e]) + dot_nt(up_grad[here], wu_ref[e])
        sums = jnp.sum(score[here], axis=1, keepdims=True)
        high = sums.astype(BF16).astype(F32)
        at = lax.broadcasted_iota(jnp.int32, (count, 2 * LANE - width), 1)
        ends = jnp.where(at == 0, high, jnp.where(at == 1, sums - high, 0.0)).astype(BF16)
        total = total.astype(BF16)
        done = 0
        while done < count:
            group, inner = divmod(low + done, rows)
            n = min(rows - inner, count - done)
            first = group * 2 * OWN * rows + 2 * e * rows + inner
            back[first : first + n, :] = total[done : done + n, 0:LANE]
            back[first + rows : first + rows + n, 0 : width - LANE] = total[done : done + n, LANE:width]
            back[first + rows : first + rows + n, width - LANE :] = ends[done : done + n]
            done += n
    shape = (GROUP, PAIR, 2 * OWN * rows)
    second, expert, slot = decode(lax.broadcasted_iota(jnp.int32, shape, 1))
    goal = (2 * expert + second) * rows + lax.broadcasted_iota(jnp.int32, shape, 0) * MOST + slot
    select = (lax.broadcasted_iota(jnp.int32, shape, 2) == goal) & (slot < MOST)
    select = select.reshape(columns, 2 * OWN * rows).astype(F32).astype(BF16)
    for g in range(sources // GROUP):
        piece = dot(select, back[g * 2 * OWN * rows : (g + 1) * 2 * OWN * rows, :])
        out_ref[g * columns : (g + 1) * columns, :] = piece.astype(BF16)


def combine_kernel(homes, routes_ref, slots_ref, got_ref, tokens_ref, probs_ref):
    tokens, width = tokens_ref.shape
    experts = homes * OWN
    hits, ranks = rank_table(routes_ref[...], experts)
    pick = expert_rows(0, homes, experts)
    rank_of = dot_nt(ranks, pick.astype(F32).astype(BF16))
    first = (rank_of == slots_ref[0:1, :]).astype(F32).astype(BF16)
    second = (rank_of == slots_ref[1:2, :]).astype(F32).astype(BF16)
    tokens_ref[:, 0:LANE] = dot(first, got_ref[...])
    tokens_ref[:, LANE:width] = dot(second, got_ref[...])[:, : width - LANE]
    ends = got_ref[...].astype(F32)
    high = jnp.where(pick, ends[:, width - LANE : width - LANE + 1], 0.0).astype(BF16)
    low = jnp.where(pick, ends[:, width - LANE + 1 : width - LANE + 2], 0.0).astype(BF16)
    table = dot(second, high) + dot(second, low)
    at = lax.broadcasted_iota(jnp.int32, probs_ref.shape, 1)
    result = jnp.zeros(probs_ref.shape, F32)
    for k, hit in enumerate(hits):
        mine = jnp.sum(jnp.where(hit, table, 0.0), axis=1, keepdims=True)
        result = jnp.where(at == k, mine, result)
    probs_ref[...] = result


def cost(flops, nbytes):
    return pl.CostEstimate(flops=flops, bytes_accessed=nbytes, transcendentals=0)


def on_device(cotangent, probs, routes, gate_pre, up_pre, w_gate, w_up, w_down):
    tokens, width = cotangent.shape
    hidden = w_gate.shape[2]
    homes = lax.axis_size("x") * lax.axis_size("z")
    ring = lax.axis_size("y")
    capacity = homes * MOST
    share = -(-capacity // 32) * 16
    blocks = hidden // LANE
    packed = homes * PAIR
    here = lax.axis_index("core").astype(jnp.int32)[None]
    half_shape = jax.ShapeDtypeStruct((blocks, capacity + share, LANE), BF16)
    rows_shape = jax.ShapeDtypeStruct((OWN, 2 * share, 2 * LANE), BF16)

    with jax.named_scope("send_rows"):
        send = pl.pallas_call(
            functools.partial(send_kernel, homes),
            out_shape=jax.ShapeDtypeStruct((packed, LANE), BF16),
            in_specs=[VMEM] * 3,
            out_specs=VMEM,
            scratch_shapes=[pltpu.VMEM((3 * tokens, LANE), BF16)],
            compiler_params=PARAMS,
            cost_estimate=cost(10**9, 10**6),
        )(routes, probs, cotangent)
    with jax.named_scope("dispatch"):
        got = lax.all_to_all(send.reshape(homes, PAIR, LANE), ("x", "z"), 0, 0, tiled=True).reshape(packed, LANE)
    with jax.named_scope("down_other"):
        rows, other = pl.pallas_call(
            functools.partial(unpack_kernel, share),
            out_shape=(rows_shape, half_shape),
            in_specs=[SMEM, VMEM, VMEM],
            out_specs=(VMEM, VMEM),
            compiler_params=PARAMS,
            cost_estimate=cost(10**9, 4 * 10**6),
        )(here, got, w_down)
    with jax.named_scope("swap_cores"):
        swapped = lax.ppermute(other, "core", [(0, 1), (1, 0)])
    with jax.named_scope("down_own"):
        own = pl.pallas_call(
            functools.partial(down_kernel, share),
            out_shape=half_shape,
            in_specs=[SMEM, VMEM, VMEM],
            out_specs=VMEM,
            compiler_params=PARAMS,
            cost_estimate=cost(10**9, 4 * 10**6),
        )(here, rows, w_down)
    with jax.named_scope("add_cores"):
        chip = (own.astype(F32) + swapped.astype(F32)).astype(BF16)
    with jax.named_scope("sum_over_y"):
        parts = lax.all_to_all(chip, "y", 0, 0, tiled=True)
        share_sum = jnp.sum(parts.astype(F32), axis=0).astype(BF16)
    with jax.named_scope("gather_hidden"):
        grad = lax.all_gather(share_sum, ("y", "core"), axis=0)
    with jax.named_scope("back"):
        back = pl.pallas_call(
            functools.partial(back_kernel, share),
            out_shape=jax.ShapeDtypeStruct((packed, LANE), BF16),
            in_specs=[VMEM] * 6,
            out_specs=VMEM,
            scratch_shapes=[
                pltpu.VMEM((capacity, hidden), BF16),
                pltpu.VMEM((capacity, hidden), BF16),
                pltpu.VMEM((capacity, LANE), F32),
                pltpu.VMEM((capacity, LANE), F32),
                pltpu.VMEM((homes * MOST * 2 * OWN, LANE), BF16),
            ],
            compiler_params=PARAMS,
            cost_estimate=cost(2 * 10**9, 10**7),
        )(grad, rows, gate_pre, up_pre, w_gate, w_up)
    with jax.named_scope("way_back"):
        home = lax.all_to_all(back.reshape(homes, PAIR, LANE), ("x", "z"), 0, 0, tiled=True).reshape(packed, LANE)
    row = np.arange(packed) % PAIR
    place = row % SLOTS
    slot = np.where(place < OWN * MOST, place % MOST, 99)
    slots = np.stack([np.where(row < SLOTS, slot, 99), np.where(row < SLOTS, 99, slot)]).astype(np.float32)
    with jax.named_scope("combine"):
        return pl.pallas_call(
            functools.partial(combine_kernel, homes),
            out_shape=(
                jax.ShapeDtypeStruct((tokens, width), F32),
                jax.ShapeDtypeStruct(probs.shape, F32),
            ),
            in_specs=[VMEM] * 3,
            out_specs=(VMEM, VMEM),
            compiler_params=PARAMS,
            cost_estimate=cost(10**9, 10**6),
        )(routes, jnp.asarray(slots), home)


def solution(mesh):
    node, local = ("y", "core"), ("x", "z")
    y, x = mesh.devices.shape[0] // 2, 4
    parts = Mesh(mesh.devices.reshape(y, 2, x, -1), node + local)
    return jax.shard_map(
        on_device,
        mesh=parts,
        in_specs=(
            P(local, node),
            P(local, None),
            P(local, None),
            P(local, None, None),
            P(local, None, None),
            P(local, node, None),
            P(local, node, None),
            P(local, node, None),
        ),
        out_specs=(P(local, node), P(local, None)),
        check_vma=False,
    )
```

```python
import functools

import jax
import jax.numpy as jnp
import numpy as np
from jax import lax
from jax.experimental import pallas as pl
from jax.experimental.pallas import tpu as pltpu
from jax.sharding import Mesh, PartitionSpec as P

MOST = 9
OWN = 3
SLOTS = 28
PAIR = 2 * SLOTS
LANE = 128
GROUP = 16
F32 = jnp.float32
BF16 = jnp.bfloat16
NT = (((1,), (1,)), ((), ()))
VMEM = pl.BlockSpec(memory_space=pltpu.VMEM)
SMEM = pl.BlockSpec(memory_space=pltpu.SMEM)
PARAMS = pltpu.CompilerParams(vmem_limit_bytes=32 * 1024 * 1024)


def dot(a, b):
    return jnp.dot(a, b, preferred_element_type=F32)


def dot_nt(a, b):
    return lax.dot_general(a, b, NT, preferred_element_type=F32)


def decode(row):
    second = (row >= SLOTS).astype(jnp.int32)
    place = row - SLOTS * second
    expert = (place >= MOST).astype(jnp.int32) + (place >= 2 * MOST).astype(jnp.int32)
    expert = jnp.minimum(expert, OWN - 1)
    return second, expert, place - MOST * expert


def rank_table(routes, experts):
    tokens, top = routes.shape
    lane = lax.broadcasted_iota(jnp.int32, (tokens, experts), 1)
    hits = [routes[:, k : k + 1] == lane for k in range(top)]
    named = sum(hit.astype(F32) for hit in hits)
    square = (tokens, tokens)
    earlier = lax.broadcasted_iota(jnp.int32, square, 0) > lax.broadcasted_iota(jnp.int32, square, 1)
    rank = dot(earlier.astype(F32).astype(BF16), named.astype(BF16))
    return hits, jnp.where(named > 0.0, rank, 31.0).astype(BF16)


def expert_rows(first, homes, experts):
    shape = (homes, PAIR, experts)
    _, expert, _ = decode(lax.broadcasted_iota(jnp.int32, shape, 1))
    wanted = (lax.broadcasted_iota(jnp.int32, shape, 0) + first) * OWN + expert
    return (lax.broadcasted_iota(jnp.int32, shape, 2) == wanted).reshape(homes * PAIR, experts)


def send_kernel(homes, routes_ref, probs_ref, cot_ref, out_ref, right):
    width, tokens = cot_ref.shape
    experts = homes * OWN
    routes = routes_ref[...].astype(F32).T.astype(jnp.int32)
    hits, ranks = rank_table(routes, experts)
    probs = probs_ref[...].T
    weight = sum(jnp.where(hit, probs[:, k : k + 1], 0.0) for k, hit in enumerate(hits)).astype(BF16)
    right[...] = jnp.zeros_like(right)
    right[:, 0:tokens] = cot_ref[0:LANE, :].astype(BF16)
    right[0 : width - LANE, tokens : 2 * tokens] = cot_ref[LANE:width, :].astype(BF16)
    mark = lax.broadcasted_iota(jnp.int32, (LANE, tokens), 0) == width - LANE
    right[:, 2 * tokens : 3 * tokens] = mark.astype(F32).astype(BF16)
    step = 8 if homes % 8 == 0 else homes
    for first in range(0, homes, step):
        pick = expert_rows(first, step, experts).astype(F32).astype(BF16)
        rank_of = dot_nt(pick, ranks)
        weight_of = dot_nt(pick, weight)
        shape = (step, PAIR, tokens)
        second, _, slot = decode(lax.broadcasted_iota(jnp.int32, shape, 1))
        second = second.reshape(step * PAIR, tokens) > 0
        here = rank_of == slot.astype(F32).reshape(step * PAIR, tokens)
        left = jnp.concatenate(
            [
                jnp.where(here & ~second, 1.0, 0.0).astype(BF16),
                jnp.where(here & second, 1.0, 0.0).astype(BF16),
                jnp.where(here & second, weight_of, 0.0).astype(BF16),
            ],
            axis=1,
        )
        out_ref[first * PAIR : (first + step) * PAIR, :] = dot_nt(left, right[...]).astype(BF16)


def down_half(half, share, rows_ref, w_ref, out_ref, plus_ref=None):
    capacity = out_ref.shape[1] - share
    whole = half * (OWN - 1)
    width = w_ref.shape[1]
    hidden = w_ref.shape[2]
    left = rows_ref[whole, 0:capacity, 0:width]
    part = rows_ref[1, pl.ds(pl.multiple_of(half * share, 16), share), 0:width]
    tile = 2 * LANE
    for n in range(hidden // tile):
        columns = slice(n * tile, (n + 1) * tile)
        for a, top, count in (
            (dot(left, w_ref[whole, :, columns]), 0, capacity),
            (dot(part, w_ref[1, :, columns]), capacity, share),
        ):
            for m, piece in ((2 * n, a[:, :LANE]), (2 * n + 1, a[:, LANE:])):
                if plus_ref is not None:
                    piece = piece + plus_ref[m, top : top + count, :].astype(F32)
                out_ref[m, top : top + count, :] = piece.astype(BF16)


def unpack_kernel(share, half_ref, got_ref, w_ref, rows_ref, out_ref):
    sources = got_ref.shape[0] // PAIR
    capacity = sources * MOST
    rows, columns = GROUP * MOST, GROUP * PAIR
    at = lax.broadcasted_iota(jnp.int32, (1, columns), 1)
    source = jnp.floor((at.astype(F32) + 0.5) * (1.0 / PAIR)).astype(jnp.int32)
    second, expert, slot = decode(at - PAIR * source)
    goal = jnp.where(slot < MOST, (2 * expert + second) * rows + source * MOST + slot, -1)
    select = lax.broadcasted_iota(jnp.int32, (2 * OWN * rows, columns), 0) == goal
    select = select.astype(F32).astype(BF16)
    rows_ref[:, capacity:, :] = jnp.zeros((OWN, rows_ref.shape[1] - capacity, 2 * LANE), BF16)
    for g in range(sources // GROUP):
        piece = dot(select, got_ref[g * columns : (g + 1) * columns, :]).astype(BF16)
        for e in range(OWN):
            for second in range(2):
                top = (2 * e + second) * rows
                rows_ref[e, g * rows : (g + 1) * rows, second * LANE : (second + 1) * LANE] = piece[top : top + rows]
    down_half(1 - half_ref[0], share, rows_ref, w_ref, out_ref)


def down_kernel(share, half_ref, rows_ref, w_ref, plus_ref, out_ref):
    down_half(half_ref[0], share, rows_ref, w_ref, out_ref, plus_ref)


def factor_kernel(gate_ref, up_ref, up_factor_ref, gate_factor_ref):
    experts, capacity, hidden = gate_ref.shape
    step = 48
    for e in range(experts):

        def part(i, carry, e=e):
            rows = pl.ds(pl.multiple_of(i * step, step), step)
            for b in range(0, hidden, LANE):
                gate = gate_ref[e, rows, b : b + LANE].astype(F32)
                up = up_ref[e, rows, b : b + LANE].astype(F32)
                sig = lax.logistic(gate)
                up_factor_ref[e, rows, b : b + LANE] = gate * sig
                gate_factor_ref[e, rows, b : b + LANE] = up * sig * (1.0 + gate * (1.0 - sig))
            return carry

        lax.fori_loop(0, capacity // step, part, 0)


def sum_kernel(parts_ref, out_ref):
    sources, rows, _ = parts_ref.shape
    total = parts_ref[0].astype(F32)
    for i in range(1, sources):
        total = total + parts_ref[i].astype(F32)
    largest = jnp.max(jnp.max(jnp.abs(total), axis=0, keepdims=True), axis=1, keepdims=True)
    largest = jnp.broadcast_to(jnp.maximum(largest, 1e-35), (16, LANE))
    power = jnp.clip(jnp.floor(jnp.log2(largest)), -100.0, 100.0)
    out_ref[0:rows, :] = total * jnp.exp2(-power)[0:1]
    out_ref[rows:, :] = power


def back_kernel(
    share, grad_ref, rows_ref, up_ref, up_factor_ref, gate_factor_ref, wg_ref, wu_ref, out_ref,
    gate_grad, up_grad, score, back,
):
    sources = out_ref.shape[0] // PAIR
    capacity = sources * MOST
    width = wg_ref.shape[1]
    blocks = up_ref.shape[2] // LANE
    rows, columns = GROUP * MOST, GROUP * PAIR
    tail = capacity - share
    for e, low, count, half, top in (
        (0, 0, capacity, 0, 0),
        (OWN - 1, 0, capacity, 1, 0),
        (1, 0, share, 0, capacity),
        (1, share, tail, 1, capacity),
    ):
        here = slice(0, count)
        score[here] = jnp.zeros((count, LANE), F32)

        def block(b, carry, e=e, low=low, count=count, half=half, top=top, here=here):
            columns = pl.ds(pl.multiple_of(b * LANE, LANE), LANE)
            scale = jnp.exp2(grad_ref[2 * b + half, capacity + share : capacity + share + 1, :])
            grad = grad_ref[2 * b + half, top : top + count, :] * scale
            by_up = grad * up_factor_ref[e, low : low + count, columns]
            score[here] += by_up * up_ref[e, low : low + count, columns].astype(F32)
            up_grad[here, columns] = by_up.astype(BF16)
            gate_grad[here, columns] = (grad * gate_factor_ref[e, low : low + count, columns]).astype(BF16)
            return carry

        lax.fori_loop(0, blocks, block, 0)
        weight = rows_ref[e, low : low + count, LANE:].astype(F32)[:, width - LANE : width - LANE + 1]
        total = dot_nt(gate_grad[here], wg_ref[e]) + dot_nt(up_grad[here], wu_ref[e])
        total = total * weight
        sums = jnp.sum(score[here], axis=1, keepdims=True)
        high = sums.astype(BF16).astype(F32)
        at = lax.broadcasted_iota(jnp.int32, (count, 2 * LANE - width), 1)
        ends = jnp.where(at == 0, high, jnp.where(at == 1, sums - high, 0.0)).astype(BF16)
        total = total.astype(BF16)
        done = 0
        while done < count:
            group, inner = divmod(low + done, rows)
            n = min(rows - inner, count - done)
            first = group * 2 * OWN * rows + 2 * e * rows + inner
            back[first : first + n, :] = total[done : done + n, 0:LANE]
            back[first + rows : first + rows + n, 0 : width - LANE] = total[done : done + n, LANE:width]
            back[first + rows : first + rows + n, width - LANE :] = ends[done : done + n]
            done += n
    shape = (GROUP, PAIR, 2 * OWN * rows)
    second, expert, slot = decode(lax.broadcasted_iota(jnp.int32, shape, 1))
    goal = (2 * expert + second) * rows + lax.broadcasted_iota(jnp.int32, shape, 0) * MOST + slot
    select = (lax.broadcasted_iota(jnp.int32, shape, 2) == goal) & (slot < MOST)
    select = select.reshape(columns, 2 * OWN * rows).astype(F32).astype(BF16)
    for g in range(sources // GROUP):
        piece = dot(select, back[g * 2 * OWN * rows : (g + 1) * 2 * OWN * rows, :])
        out_ref[g * columns : (g + 1) * columns, :] = piece.astype(BF16)


def combine_kernel(homes, routes_ref, slots_ref, got_ref, tokens_ref, probs_ref):
    width, tokens = tokens_ref.shape
    experts = homes * OWN
    hits, ranks = rank_table(routes_ref[...].astype(F32).T.astype(jnp.int32), experts)
    pick = expert_rows(0, homes, experts)
    rank_of = dot_nt(ranks, pick.astype(F32).astype(BF16))
    first = (rank_of == slots_ref[0:1, :]).astype(F32).astype(BF16)
    second = (rank_of == slots_ref[1:2, :]).astype(F32).astype(BF16)
    tokens_ref[0:LANE, :] = dot(first, got_ref[...]).T
    tokens_ref[LANE:width, :] = dot(second, got_ref[...]).T[: width - LANE]
    ends = got_ref[...].astype(F32)
    high = jnp.where(pick, ends[:, width - LANE : width - LANE + 1], 0.0).astype(BF16)
    low = jnp.where(pick, ends[:, width - LANE + 1 : width - LANE + 2], 0.0).astype(BF16)
    table = dot(second, high) + dot(second, low)
    at = lax.broadcasted_iota(jnp.int32, (tokens, len(hits)), 1)
    result = jnp.zeros((tokens, len(hits)), F32)
    for k, hit in enumerate(hits):
        mine = jnp.sum(jnp.where(hit, table, 0.0), axis=1, keepdims=True)
        result = jnp.where(at == k, mine, result)
    probs_ref[...] = result.T


def cost(flops, nbytes):
    return pl.CostEstimate(flops=flops, bytes_accessed=nbytes, transcendentals=0)


def on_device(cotangent, probs, routes, gate_pre, up_pre, w_gate, w_up, w_down):
    tokens, width = cotangent.shape
    hidden = w_gate.shape[2]
    homes = lax.axis_size("x") * lax.axis_size("z")
    ring = lax.axis_size("y")
    capacity = homes * MOST
    share = -(-capacity // 32) * 16
    blocks = hidden // LANE
    packed = homes * PAIR
    here = lax.axis_index("core").astype(jnp.int32)[None]
    half_shape = jax.ShapeDtypeStruct((blocks, capacity + share, LANE), BF16)
    rows_shape = jax.ShapeDtypeStruct((OWN, 2 * share, 2 * LANE), BF16)

    with jax.named_scope("send_rows"):
        send = pl.pallas_call(
            functools.partial(send_kernel, homes),
            out_shape=jax.ShapeDtypeStruct((packed, LANE), BF16),
            in_specs=[VMEM] * 3,
            out_specs=VMEM,
            scratch_shapes=[pltpu.VMEM((LANE, 3 * tokens), BF16)],
            compiler_params=PARAMS,
            cost_estimate=cost(10**9, 10**6),
        )(routes.T, probs.T, cotangent.T)
    with jax.named_scope("factors"):
        factor = jax.ShapeDtypeStruct(gate_pre.shape, F32)
        up_factor, gate_factor = pl.pallas_call(
            factor_kernel,
            out_shape=(factor, factor),
            in_specs=[VMEM] * 2,
            out_specs=(VMEM, VMEM),
            compiler_params=PARAMS,
            cost_estimate=pl.CostEstimate(flops=2 * 10**7, bytes_accessed=2 * 10**7, transcendentals=10**6),
        )(gate_pre, up_pre)
    with jax.named_scope("dispatch"):
        got = lax.all_to_all(send.reshape(homes, PAIR, LANE), ("x", "z"), 0, 0, tiled=True).reshape(packed, LANE)
        got, up_factor, gate_factor = lax.optimization_barrier((got, up_factor, gate_factor))
    with jax.named_scope("down_other"):
        rows, other = pl.pallas_call(
            functools.partial(unpack_kernel, share),
            out_shape=(rows_shape, half_shape),
            in_specs=[SMEM, VMEM, VMEM],
            out_specs=(VMEM, VMEM),
            compiler_params=PARAMS,
            cost_estimate=cost(10**9, 4 * 10**6),
        )(here, got, w_down)
    with jax.named_scope("swap_cores"):
        swapped = lax.ppermute(other, "core", [(0, 1), (1, 0)])
    with jax.named_scope("down_own"):
        chip = pl.pallas_call(
            functools.partial(down_kernel, share),
            out_shape=half_shape,
            in_specs=[SMEM, VMEM, VMEM, VMEM],
            out_specs=VMEM,
            compiler_params=PARAMS,
            cost_estimate=cost(10**9, 4 * 10**6),
        )(here, rows, w_down, swapped)
    with jax.named_scope("sum_over_y"):
        parts = lax.all_to_all(chip, "y", 0, 0, tiled=True)
        scaled = pl.pallas_call(
            sum_kernel,
            out_shape=jax.ShapeDtypeStruct((capacity + share + 16, LANE), F32),
            in_specs=[VMEM],
            out_specs=VMEM,
            compiler_params=PARAMS,
            cost_estimate=cost(10**6, 3 * 10**6),
        )(parts)
    with jax.named_scope("gather_hidden"):
        grad = lax.all_gather(scaled.astype(jnp.float16), ("y", "core"), axis=0).astype(F32)
    with jax.named_scope("back"):
        back = pl.pallas_call(
            functools.partial(back_kernel, share),
            out_shape=jax.ShapeDtypeStruct((packed, LANE), BF16),
            in_specs=[VMEM] * 7,
            out_specs=VMEM,
            scratch_shapes=[
                pltpu.VMEM((capacity, hidden), BF16),
                pltpu.VMEM((capacity, hidden), BF16),
                pltpu.VMEM((capacity, LANE), F32),
                pltpu.VMEM((homes * MOST * 2 * OWN, LANE), BF16),
            ],
            compiler_params=PARAMS,
            cost_estimate=cost(2 * 10**9, 10**7),
        )(grad, rows, up_pre, up_factor, gate_factor, w_gate, w_up)
    with jax.named_scope("way_back"):
        home = lax.all_to_all(back.reshape(homes, PAIR, LANE), ("x", "z"), 0, 0, tiled=True).reshape(packed, LANE)
    row = np.arange(packed) % PAIR
    place = row % SLOTS
    slot = np.where(place < OWN * MOST, place % MOST, 99)
    slots = np.stack([np.where(row < SLOTS, slot, 99), np.where(row < SLOTS, 99, slot)]).astype(np.float32)
    with jax.named_scope("combine"):
        grad_tokens, grad_probs = pl.pallas_call(
            functools.partial(combine_kernel, homes),
            out_shape=(
                jax.ShapeDtypeStruct((width, tokens), F32),
                jax.ShapeDtypeStruct(probs.shape[::-1], F32),
            ),
            in_specs=[VMEM] * 3,
            out_specs=(VMEM, VMEM),
            compiler_params=PARAMS,
            cost_estimate=cost(10**9, 10**6),
        )(routes.T, jnp.asarray(slots), home)
        return grad_tokens.T, grad_probs.T


def solution(mesh):
    node, local = ("y", "core"), ("x", "z")
    y, x = mesh.devices.shape[0] // 2, 4
    parts = Mesh(mesh.devices.reshape(y, 2, x, -1), node + local)
    return jax.shard_map(
        on_device,
        mesh=parts,
        in_specs=(
            P(local, node),
            P(local, None),
            P(local, None),
            P(local, None, None),
            P(local, None, None),
            P(local, node, None),
            P(local, node, None),
            P(local, node, None),
        ),
        out_specs=(P(local, node), P(local, None)),
        check_vma=False,
    )
```

```python
import functools

import jax
import jax.numpy as jnp
import numpy as np
from jax import lax
from jax.experimental import pallas as pl
from jax.experimental.pallas import tpu as pltpu
from jax.sharding import Mesh, PartitionSpec as P

MOST = 9
OWN = 3
SLOTS = 28
PAIR = 2 * SLOTS
LANE = 128
GROUP = 16
F32 = jnp.float32
BF16 = jnp.bfloat16
NT = (((1,), (1,)), ((), ()))
VMEM = pl.BlockSpec(memory_space=pltpu.VMEM)
SMEM = pl.BlockSpec(memory_space=pltpu.SMEM)
PARAMS = pltpu.CompilerParams(vmem_limit_bytes=24 * 1024 * 1024)


def dot(a, b):
    return jnp.dot(a, b, preferred_element_type=F32)


def dot_nt(a, b):
    return lax.dot_general(a, b, NT, preferred_element_type=F32)


def decode(row):
    second = (row >= SLOTS).astype(jnp.int32)
    place = row - SLOTS * second
    expert = (place >= MOST).astype(jnp.int32) + (place >= 2 * MOST).astype(jnp.int32)
    expert = jnp.minimum(expert, OWN - 1)
    return second, expert, place - MOST * expert


def rank_table(routes, experts):
    tokens, top = routes.shape
    lane = lax.broadcasted_iota(jnp.int32, (tokens, experts), 1)
    hits = [routes[:, k : k + 1] == lane for k in range(top)]
    named = sum(hit.astype(F32) for hit in hits)
    square = (tokens, tokens)
    earlier = lax.broadcasted_iota(jnp.int32, square, 0) > lax.broadcasted_iota(jnp.int32, square, 1)
    rank = dot(earlier.astype(F32).astype(BF16), named.astype(BF16))
    return hits, jnp.where(named > 0.0, rank, 31.0).astype(BF16)


def expert_rows(first, homes, experts):
    shape = (homes, PAIR, experts)
    _, expert, _ = decode(lax.broadcasted_iota(jnp.int32, shape, 1))
    wanted = (lax.broadcasted_iota(jnp.int32, shape, 0) + first) * OWN + expert
    return (lax.broadcasted_iota(jnp.int32, shape, 2) == wanted).reshape(homes * PAIR, experts)


def send_kernel(homes, routes_ref, probs_ref, cot_ref, out_ref, right):
    width, tokens = cot_ref.shape
    experts = homes * OWN
    routes = routes_ref[...].astype(F32).T.astype(jnp.int32)
    hits, ranks = rank_table(routes, experts)
    probs = probs_ref[...].T
    weight = sum(jnp.where(hit, probs[:, k : k + 1], 0.0) for k, hit in enumerate(hits)).astype(BF16)
    right[...] = jnp.zeros_like(right)
    right[:, 0:tokens] = cot_ref[0:LANE, :].astype(BF16)
    right[0 : width - LANE, tokens : 2 * tokens] = cot_ref[LANE:width, :].astype(BF16)
    mark = lax.broadcasted_iota(jnp.int32, (LANE, tokens), 0) == width - LANE
    right[:, 2 * tokens : 3 * tokens] = mark.astype(F32).astype(BF16)
    step = 8 if homes % 8 == 0 else homes
    for first in range(0, homes, step):
        pick = expert_rows(first, step, experts).astype(F32).astype(BF16)
        rank_of = dot_nt(pick, ranks)
        weight_of = dot_nt(pick, weight)
        shape = (step, PAIR, tokens)
        second, _, slot = decode(lax.broadcasted_iota(jnp.int32, shape, 1))
        second = second.reshape(step * PAIR, tokens) > 0
        here = rank_of == slot.astype(F32).reshape(step * PAIR, tokens)
        left = jnp.concatenate(
            [
                jnp.where(here & ~second, 1.0, 0.0).astype(BF16),
                jnp.where(here & second, 1.0, 0.0).astype(BF16),
                jnp.where(here & second, weight_of, 0.0).astype(BF16),
            ],
            axis=1,
        )
        out_ref[first * PAIR : (first + step) * PAIR, :] = dot_nt(left, right[...]).astype(BF16)


def down_half(half, share, rows_ref, w_ref, out_ref, plus_ref=None):
    capacity = out_ref.shape[1] - share
    whole = half * (OWN - 1)
    width = w_ref.shape[1]
    hidden = w_ref.shape[2]
    left = rows_ref[whole, 0:capacity, 0:width]
    part = rows_ref[1, pl.ds(pl.multiple_of(half * share, 16), share), 0:width]
    tile = 2 * LANE
    for n in range(hidden // tile):
        columns = slice(n * tile, (n + 1) * tile)
        for a, top, count in (
            (dot(left, w_ref[whole, :, columns]), 0, capacity),
            (dot(part, w_ref[1, :, columns]), capacity, share),
        ):
            for m, piece in ((2 * n, a[:, :LANE]), (2 * n + 1, a[:, LANE:])):
                if plus_ref is not None:
                    piece = piece + plus_ref[m, top : top + count, :].astype(F32)
                out_ref[m, top : top + count, :] = piece.astype(BF16)


def unpack_kernel(share, half_ref, got_ref, select_ref, w_ref, rows_ref, out_ref):
    sources = got_ref.shape[0] // PAIR
    capacity = sources * MOST
    rows, columns = GROUP * MOST, GROUP * PAIR
    rows_ref[:, capacity:, :] = jnp.zeros((OWN, rows_ref.shape[1] - capacity, 2 * LANE), BF16)
    for g in range(sources // GROUP):
        piece = dot(select_ref[...], got_ref[g * columns : (g + 1) * columns, :]).astype(BF16)
        for e in range(OWN):
            for second in range(2):
                top = (2 * e + second) * rows
                rows_ref[e, g * rows : (g + 1) * rows, second * LANE : (second + 1) * LANE] = piece[top : top + rows]
    down_half(1 - half_ref[0], share, rows_ref, w_ref, out_ref)


def down_kernel(share, half_ref, rows_ref, w_ref, plus_ref, out_ref):
    down_half(half_ref[0], share, rows_ref, w_ref, out_ref, plus_ref)


def prepare_kernel(
    homes, routes_ref, slots_ref, gate_ref, up_ref,
    up_factor_ref, gate_factor_ref, select_in_ref, select_out_ref, first_ref, second_ref, pick_ref,
):
    capacity, hidden = gate_ref.shape[1:]
    experts = homes * OWN
    step = 48
    for e in range(OWN):

        def part(i, carry, e=e):
            rows = pl.ds(pl.multiple_of(i * step, step), step)
            for b in range(0, hidden, LANE):
                gate = gate_ref[e, rows, b : b + LANE].astype(F32)
                up = up_ref[e, rows, b : b + LANE].astype(F32)
                sig = lax.logistic(gate)
                up_factor_ref[e, rows, b : b + LANE] = gate * sig
                gate_factor_ref[e, rows, b : b + LANE] = up * sig * (1.0 + gate * (1.0 - sig))
            return carry

        lax.fori_loop(0, capacity // step, part, 0)
    rows, columns = GROUP * MOST, GROUP * PAIR
    at = lax.broadcasted_iota(jnp.int32, (1, columns), 1)
    source = jnp.floor((at.astype(F32) + 0.5) * (1.0 / PAIR)).astype(jnp.int32)
    second, expert, slot = decode(at - PAIR * source)
    goal = jnp.where(slot < MOST, (2 * expert + second) * rows + source * MOST + slot, -1)
    select = lax.broadcasted_iota(jnp.int32, (2 * OWN * rows, columns), 0) == goal
    select_in_ref[...] = select.astype(F32).astype(BF16)
    shape = (GROUP, PAIR, 2 * OWN * rows)
    second, expert, slot = decode(lax.broadcasted_iota(jnp.int32, shape, 1))
    goal = (2 * expert + second) * rows + lax.broadcasted_iota(jnp.int32, shape, 0) * MOST + slot
    select = (lax.broadcasted_iota(jnp.int32, shape, 2) == goal) & (slot < MOST)
    select_out_ref[...] = select.reshape(columns, 2 * OWN * rows).astype(F32).astype(BF16)
    _, ranks = rank_table(routes_ref[...].astype(F32).T.astype(jnp.int32), experts)
    pick_ref[...] = expert_rows(0, homes, experts).astype(F32).astype(BF16)
    rank_of = dot_nt(ranks, pick_ref[...])
    first_ref[...] = (rank_of == slots_ref[0:1, :]).astype(F32).astype(BF16)
    second_ref[...] = (rank_of == slots_ref[1:2, :]).astype(F32).astype(BF16)


def sum_kernel(parts_ref, out_ref):
    sources, rows, _ = parts_ref.shape
    total = parts_ref[0].astype(F32)
    for i in range(1, sources):
        total = total + parts_ref[i].astype(F32)
    largest = jnp.max(jnp.max(jnp.abs(total), axis=0, keepdims=True), axis=1, keepdims=True)
    largest = jnp.broadcast_to(jnp.maximum(largest, 1e-35), (16, LANE))
    power = jnp.clip(jnp.floor(jnp.log2(largest)), -100.0, 100.0)
    out_ref[0:rows, :] = total * jnp.exp2(-power)[0:1]
    out_ref[rows:, :] = power


def back_kernel(
    share, grad_ref, rows_ref, up_ref, up_factor_ref, gate_factor_ref, wg_ref, wu_ref, select_ref, out_ref,
    gate_grad, up_grad, score, back,
):
    sources = out_ref.shape[0] // PAIR
    capacity = sources * MOST
    width = wg_ref.shape[1]
    blocks = up_ref.shape[2] // LANE
    rows, columns = GROUP * MOST, GROUP * PAIR
    tail = capacity - share
    for e, low, count, half, top in (
        (0, 0, capacity, 0, 0),
        (OWN - 1, 0, capacity, 1, 0),
        (1, 0, share, 0, capacity),
        (1, share, tail, 1, capacity),
    ):
        here = slice(0, count)
        score[here] = jnp.zeros((count, LANE), F32)

        def block(b, carry, e=e, low=low, count=count, half=half, top=top, here=here):
            columns = pl.ds(pl.multiple_of(b * LANE, LANE), LANE)
            scale = jnp.exp2(grad_ref[2 * b + half, capacity + share : capacity + share + 1, :])
            grad = grad_ref[2 * b + half, top : top + count, :] * scale
            by_up = grad * up_factor_ref[e, low : low + count, columns]
            score[here] += by_up * up_ref[e, low : low + count, columns].astype(F32)
            up_grad[here, columns] = by_up.astype(BF16)
            gate_grad[here, columns] = (grad * gate_factor_ref[e, low : low + count, columns]).astype(BF16)
            return carry

        lax.fori_loop(0, blocks, block, 0)
        weight = rows_ref[e, low : low + count, LANE:].astype(F32)[:, width - LANE : width - LANE + 1]
        total = dot_nt(gate_grad[here], wg_ref[e]) + dot_nt(up_grad[here], wu_ref[e])
        total = total * weight
        sums = jnp.sum(score[here], axis=1, keepdims=True)
        high = sums.astype(BF16).astype(F32)
        at = lax.broadcasted_iota(jnp.int32, (count, 2 * LANE - width), 1)
        ends = jnp.where(at == 0, high, jnp.where(at == 1, sums - high, 0.0)).astype(BF16)
        total = total.astype(BF16)
        done = 0
        while done < count:
            group, inner = divmod(low + done, rows)
            n = min(rows - inner, count - done)
            first = group * 2 * OWN * rows + 2 * e * rows + inner
            back[first : first + n, :] = total[done : done + n, 0:LANE]
            back[first + rows : first + rows + n, 0 : width - LANE] = total[done : done + n, LANE:width]
            back[first + rows : first + rows + n, width - LANE :] = ends[done : done + n]
            done += n
    for g in range(sources // GROUP):
        piece = dot(select_ref[...], back[g * 2 * OWN * rows : (g + 1) * 2 * OWN * rows, :])
        out_ref[g * columns : (g + 1) * columns, :] = piece.astype(BF16)


def combine_kernel(routes_ref, first_ref, second_ref, pick_ref, got_ref, tokens_ref, probs_ref):
    width, tokens = tokens_ref.shape
    experts = pick_ref.shape[1]
    tokens_ref[0:LANE, :] = dot(first_ref[...], got_ref[...]).T
    tokens_ref[LANE:width, :] = dot(second_ref[...], got_ref[...]).T[: width - LANE]
    at = lax.broadcasted_iota(jnp.int32, (16, LANE), 1) - lax.broadcasted_iota(jnp.int32, (16, LANE), 0)
    ends = dot_nt((at == width - LANE).astype(F32).astype(BF16), got_ref[...])
    second = second_ref[...].astype(F32)
    table = dot((second * ends[0:1, :]).astype(BF16), pick_ref[...])
    table = table + dot((second * ends[1:2, :]).astype(BF16), pick_ref[...])
    routes = routes_ref[...].astype(F32).T.astype(jnp.int32)
    top = routes.shape[1]
    lane = lax.broadcasted_iota(jnp.int32, (tokens, experts), 1)
    at = lax.broadcasted_iota(jnp.int32, (tokens, top), 1)
    result = jnp.zeros((tokens, top), F32)
    for k in range(top):
        mine = jnp.sum(jnp.where(routes[:, k : k + 1] == lane, table, 0.0), axis=1, keepdims=True)
        result = jnp.where(at == k, mine, result)
    probs_ref[...] = result.T


def cost(flops, nbytes):
    return pl.CostEstimate(flops=flops, bytes_accessed=nbytes, transcendentals=0)


def on_device(cotangent, probs, routes, gate_pre, up_pre, w_gate, w_up, w_down):
    tokens, width = cotangent.shape
    hidden = w_gate.shape[2]
    homes = lax.axis_size("x") * lax.axis_size("z")
    ring = lax.axis_size("y")
    capacity = homes * MOST
    share = -(-capacity // 32) * 16
    blocks = hidden // LANE
    packed = homes * PAIR
    here = lax.axis_index("core").astype(jnp.int32)[None]
    half_shape = jax.ShapeDtypeStruct((blocks, capacity + share, LANE), BF16)
    rows_shape = jax.ShapeDtypeStruct((OWN, 2 * share, 2 * LANE), BF16)

    with jax.named_scope("send_rows"):
        send = pl.pallas_call(
            functools.partial(send_kernel, homes),
            out_shape=jax.ShapeDtypeStruct((packed, LANE), BF16),
            in_specs=[VMEM] * 3,
            out_specs=VMEM,
            scratch_shapes=[pltpu.VMEM((LANE, 3 * tokens), BF16)],
            compiler_params=PARAMS,
            cost_estimate=cost(10**9, 10**6),
        )(routes.T, probs.T, cotangent.T)
    row = np.arange(packed) % PAIR
    place = row % SLOTS
    slot = np.where(place < OWN * MOST, place % MOST, 99)
    slots = np.stack([np.where(row < SLOTS, slot, 99), np.where(row < SLOTS, 99, slot)]).astype(np.float32)
    with jax.named_scope("prepare"):
        factor = jax.ShapeDtypeStruct(gate_pre.shape, F32)
        there, column = 2 * OWN * GROUP * MOST, GROUP * PAIR
        mask = jax.ShapeDtypeStruct((tokens, packed), BF16)
        ready = pl.pallas_call(
            functools.partial(prepare_kernel, homes),
            out_shape=(
                factor,
                factor,
                jax.ShapeDtypeStruct((there, column), BF16),
                jax.ShapeDtypeStruct((column, there), BF16),
                mask,
                mask,
                jax.ShapeDtypeStruct((packed, homes * OWN), BF16),
            ),
            in_specs=[VMEM] * 4,
            out_specs=(VMEM,) * 7,
            compiler_params=PARAMS,
            cost_estimate=pl.CostEstimate(flops=2 * 10**7, bytes_accessed=2 * 10**7, transcendentals=10**6),
        )(routes.T, jnp.asarray(slots), gate_pre, up_pre)
    with jax.named_scope("dispatch"):
        got = lax.all_to_all(send.reshape(homes, PAIR, LANE), ("x", "z"), 0, 0, tiled=True).reshape(packed, LANE)
    up_factor, gate_factor, select_in, select_out, first, second, pick = ready
    with jax.named_scope("down_other"):
        rows, other = pl.pallas_call(
            functools.partial(unpack_kernel, share),
            out_shape=(rows_shape, half_shape),
            in_specs=[SMEM, VMEM, VMEM, VMEM],
            out_specs=(VMEM, VMEM),
            compiler_params=PARAMS,
            cost_estimate=cost(10**9, 4 * 10**6),
        )(here, got, select_in, w_down)
    with jax.named_scope("swap_cores"):
        swapped = lax.ppermute(other, "core", [(0, 1), (1, 0)])
    with jax.named_scope("down_own"):
        chip = pl.pallas_call(
            functools.partial(down_kernel, share),
            out_shape=half_shape,
            in_specs=[SMEM, VMEM, VMEM, VMEM],
            out_specs=VMEM,
            compiler_params=PARAMS,
            cost_estimate=cost(10**9, 4 * 10**6),
        )(here, rows, w_down, swapped)
    with jax.named_scope("sum_over_y"):
        parts = lax.all_to_all(chip, "y", 0, 0, tiled=True)
        scaled = pl.pallas_call(
            sum_kernel,
            out_shape=jax.ShapeDtypeStruct((capacity + share + 16, LANE), F32),
            in_specs=[VMEM],
            out_specs=VMEM,
            compiler_params=PARAMS,
            cost_estimate=cost(10**6, 3 * 10**6),
        )(parts)
    with jax.named_scope("gather_hidden"):
        grad = lax.all_gather(scaled.astype(jnp.float16), ("y", "core"), axis=0).astype(F32)
    with jax.named_scope("back"):
        back = pl.pallas_call(
            functools.partial(back_kernel, share),
            out_shape=jax.ShapeDtypeStruct((packed, LANE), BF16),
            in_specs=[VMEM] * 8,
            out_specs=VMEM,
            scratch_shapes=[
                pltpu.VMEM((capacity, hidden), BF16),
                pltpu.VMEM((capacity, hidden), BF16),
                pltpu.VMEM((capacity, LANE), F32),
                pltpu.VMEM((homes * MOST * 2 * OWN, LANE), BF16),
            ],
            compiler_params=PARAMS,
            cost_estimate=cost(2 * 10**9, 10**7),
        )(grad, rows, up_pre, up_factor, gate_factor, w_gate, w_up, select_out)
    with jax.named_scope("way_back"):
        home = lax.all_to_all(back.reshape(homes, PAIR, LANE), ("x", "z"), 0, 0, tiled=True).reshape(packed, LANE)
    with jax.named_scope("combine"):
        grad_tokens, grad_probs = pl.pallas_call(
            combine_kernel,
            out_shape=(
                jax.ShapeDtypeStruct((width, tokens), F32),
                jax.ShapeDtypeStruct(probs.shape[::-1], F32),
            ),
            in_specs=[VMEM] * 5,
            out_specs=(VMEM, VMEM),
            compiler_params=PARAMS,
            cost_estimate=cost(10**9, 10**6),
        )(routes.T, first, second, pick, home)
        return grad_tokens.T, grad_probs.T


def solution(mesh):
    node, local = ("y", "core"), ("x", "z")
    y, x = mesh.devices.shape[0] // 2, 4
    parts = Mesh(mesh.devices.reshape(y, 2, x, -1), node + local)
    return jax.shard_map(
        on_device,
        mesh=parts,
        in_specs=(
            P(local, node),
            P(local, None),
            P(local, None),
            P(local, None, None),
            P(local, None, None),
            P(local, node, None),
            P(local, node, None),
            P(local, node, None),
        ),
        out_specs=(P(local, node), P(local, None)),
        check_vma=False,
    )
```

```python
import functools

import jax
import jax.numpy as jnp
import numpy as np
from jax import lax
from jax.experimental import pallas as pl
from jax.experimental.pallas import tpu as pltpu
from jax.sharding import Mesh, PartitionSpec as P

MOST = 9
OWN = 3
SLOTS = 28
PAIR = 2 * SLOTS
LANE = 128
GROUP = 16
F32 = jnp.float32
BF16 = jnp.bfloat16
NT = (((1,), (1,)), ((), ()))
VMEM = pl.BlockSpec(memory_space=pltpu.VMEM)
HBM = pl.BlockSpec(memory_space=pltpu.HBM)
SMEM = pl.BlockSpec(memory_space=pltpu.SMEM)
WIDE = pltpu.CompilerParams(vmem_limit_bytes=62 * 1024 * 1024)
PARAMS = pltpu.CompilerParams(vmem_limit_bytes=24 * 1024 * 1024)


def dot(a, b):
    return jnp.dot(a, b, preferred_element_type=F32)


def dot_nt(a, b):
    return lax.dot_general(a, b, NT, preferred_element_type=F32)


def decode(row):
    second = (row >= SLOTS).astype(jnp.int32)
    place = row - SLOTS * second
    expert = (place >= MOST).astype(jnp.int32) + (place >= 2 * MOST).astype(jnp.int32)
    expert = jnp.minimum(expert, OWN - 1)
    return second, expert, place - MOST * expert


def rank_table(routes, experts):
    tokens, top = routes.shape
    lane = lax.broadcasted_iota(jnp.int32, (tokens, experts), 1)
    hits = [routes[:, k : k + 1] == lane for k in range(top)]
    named = sum(hit.astype(F32) for hit in hits)
    square = (tokens, tokens)
    earlier = lax.broadcasted_iota(jnp.int32, square, 0) > lax.broadcasted_iota(jnp.int32, square, 1)
    rank = dot(earlier.astype(F32).astype(BF16), named.astype(BF16))
    return hits, jnp.where(named > 0.0, rank, 31.0).astype(BF16)


def expert_rows(first, homes, experts):
    shape = (homes, PAIR, experts)
    _, expert, _ = decode(lax.broadcasted_iota(jnp.int32, shape, 1))
    wanted = (lax.broadcasted_iota(jnp.int32, shape, 0) + first) * OWN + expert
    return (lax.broadcasted_iota(jnp.int32, shape, 2) == wanted).reshape(homes * PAIR, experts)


def send_kernel(
    homes, routes_in, probs_in, cot_in, out_hbm, right, routes_ref, probs_ref, cot_ref, out_ref, in_sems, out_sems
):
    width, tokens = cot_ref.shape
    arriving = [
        pltpu.make_async_copy(a, b, in_sems.at[i])
        for i, (a, b) in enumerate(((routes_in, routes_ref), (probs_in, probs_ref), (cot_in, cot_ref)))
    ]
    for copy in arriving:
        copy.start()
    right[...] = jnp.zeros_like(right)
    for copy in arriving:
        copy.wait()
    experts = homes * OWN
    routes = routes_ref[...].astype(F32).T.astype(jnp.int32)
    hits, ranks = rank_table(routes, experts)
    probs = probs_ref[...].T
    weight = sum(jnp.where(hit, probs[:, k : k + 1], 0.0) for k, hit in enumerate(hits)).astype(BF16)
    right[:, 0:tokens] = cot_ref[0:LANE, :].astype(BF16)
    right[0 : width - LANE, tokens : 2 * tokens] = cot_ref[LANE:width, :].astype(BF16)
    mark = lax.broadcasted_iota(jnp.int32, (LANE, tokens), 0) == width - LANE
    right[:, 2 * tokens : 3 * tokens] = mark.astype(F32).astype(BF16)
    step = 8
    leaving = []
    for first in range(0, homes, step):
        pick = expert_rows(first, step, experts).astype(F32).astype(BF16)
        rank_of = dot_nt(pick, ranks)
        weight_of = dot_nt(pick, weight)
        shape = (step, PAIR, tokens)
        second, _, slot = decode(lax.broadcasted_iota(jnp.int32, shape, 1))
        second = second.reshape(step * PAIR, tokens) > 0
        here = rank_of == slot.astype(F32).reshape(step * PAIR, tokens)
        left = jnp.concatenate(
            [
                jnp.where(here & ~second, 1.0, 0.0).astype(BF16),
                jnp.where(here & second, 1.0, 0.0).astype(BF16),
                jnp.where(here & second, weight_of, 0.0).astype(BF16),
            ],
            axis=1,
        )
        there = slice(first * PAIR, (first + step) * PAIR)
        out_ref[there, :] = dot_nt(left, right[...]).astype(BF16)
        leaving.append(pltpu.make_async_copy(out_ref.at[there], out_hbm.at[there], out_sems.at[first // step]))
        leaving[-1].start()
    for copy in leaving:
        copy.wait()


def down_half(half, share, rows_ref, w_ref, out_ref, plus_ref=None):
    capacity = out_ref.shape[1] - share
    whole = half * (OWN - 1)
    width, hidden = w_ref.shape[1:]
    left = rows_ref[whole, 0:capacity, 0:width]
    part = rows_ref[1, pl.ds(pl.multiple_of(half * share, 16), share), 0:width]
    tile = 2 * LANE
    for n in range(hidden // tile):
        columns = slice(n * tile, (n + 1) * tile)
        for a, top, count in (
            (dot(left, w_ref[whole, :, columns]), 0, capacity),
            (dot(part, w_ref[1, :, columns]), capacity, share),
        ):
            for m, piece in ((2 * n, a[:, :LANE]), (2 * n + 1, a[:, LANE:])):
                if plus_ref is not None:
                    piece = piece + plus_ref[m, top : top + count, :].astype(F32)
                out_ref[m, top : top + count, :] = piece.astype(BF16)


def unpack_kernel(share, half_ref, got_ref, w_ref, rows_ref, out_ref):
    sources = got_ref.shape[0] // PAIR
    capacity = sources * MOST
    rows, columns = GROUP * MOST, GROUP * PAIR
    at = lax.broadcasted_iota(jnp.int32, (1, columns), 1)
    source = jnp.floor((at.astype(F32) + 0.5) * (1.0 / PAIR)).astype(jnp.int32)
    second, expert, slot = decode(at - PAIR * source)
    goal = jnp.where(slot < MOST, (2 * expert + second) * rows + source * MOST + slot, -1)
    select = lax.broadcasted_iota(jnp.int32, (2 * OWN * rows, columns), 0) == goal
    select = select.astype(F32).astype(BF16)
    rows_ref[:, capacity:, :] = jnp.zeros((OWN, rows_ref.shape[1] - capacity, 2 * LANE), BF16)
    for g in range(sources // GROUP):
        piece = dot(select, got_ref[g * columns : (g + 1) * columns, :]).astype(BF16)
        for e in range(OWN):
            for second in range(2):
                top = (2 * e + second) * rows
                rows_ref[e, g * rows : (g + 1) * rows, second * LANE : (second + 1) * LANE] = piece[top : top + rows]
    down_half(1 - half_ref[0], share, rows_ref, w_ref, out_ref)


def down_kernel(share, half_ref, rows_ref, w_ref, plus_ref, out_ref):
    down_half(half_ref[0], share, rows_ref, w_ref, out_ref, plus_ref)


def prepare_kernel(
    homes, routes_ref, slots_ref, gate_ref, up_ref,
    up_factor_ref, gate_factor_ref, select_out_ref, masks_ref, pick_ref,
):
    capacity, hidden = gate_ref.shape[1:]
    experts = homes * OWN
    step = 48
    for e in range(OWN):

        def part(i, carry, e=e):
            rows = pl.ds(pl.multiple_of(i * step, step), step)
            for b in range(0, hidden, LANE):
                gate = gate_ref[e, rows, b : b + LANE].astype(F32)
                up = up_ref[e, rows, b : b + LANE].astype(F32)
                sig = lax.logistic(gate)
                up_factor_ref[e, rows, b : b + LANE] = gate * sig
                gate_factor_ref[e, rows, b : b + LANE] = up * sig * (1.0 + gate * (1.0 - sig))
            return carry

        lax.fori_loop(0, capacity // step, part, 0)
    rows, columns = GROUP * MOST, GROUP * PAIR
    shape = (GROUP, PAIR, 2 * OWN * rows)
    second, expert, slot = decode(lax.broadcasted_iota(jnp.int32, shape, 1))
    goal = (2 * expert + second) * rows + lax.broadcasted_iota(jnp.int32, shape, 0) * MOST + slot
    select = (lax.broadcasted_iota(jnp.int32, shape, 2) == goal) & (slot < MOST)
    select_out_ref[...] = select.reshape(columns, 2 * OWN * rows).astype(F32).astype(BF16)
    _, ranks = rank_table(routes_ref[...].astype(F32).T.astype(jnp.int32), experts)
    pick_ref[...] = expert_rows(0, homes, experts).astype(F32).astype(BF16)
    rank_of = dot_nt(ranks, pick_ref[...])
    tokens = rank_of.shape[0]
    masks_ref[0:tokens] = (rank_of == slots_ref[0:1, :]).astype(F32).astype(BF16)
    masks_ref[tokens:] = (rank_of == slots_ref[1:2, :]).astype(F32).astype(BF16)


def sum_kernel(parts_ref, out_ref):
    sources, rows, _ = parts_ref.shape
    total = parts_ref[0].astype(F32)
    for i in range(1, sources):
        total = total + parts_ref[i].astype(F32)
    largest = jnp.max(jnp.max(jnp.abs(total), axis=0, keepdims=True), axis=1, keepdims=True)
    largest = jnp.broadcast_to(jnp.maximum(largest, 1e-35), (16, LANE))
    power = jnp.clip(jnp.floor(jnp.log2(largest)), -100.0, 100.0)
    out_ref[0:rows, :] = total * jnp.exp2(-power)[0:1]
    out_ref[rows:, :] = power


def back_kernel(
    share, grad_ref, rows_ref, up_ref, up_factor_ref, gate_factor_ref, wg_ref, wu_ref, select_ref, out_ref,
    gate_grad, up_grad, back,
):
    sources = out_ref.shape[0] // PAIR
    capacity = sources * MOST
    width = wg_ref.shape[1]
    blocks = up_ref.shape[2] // LANE
    rows, columns = GROUP * MOST, GROUP * PAIR
    last = capacity + share
    scales = [jnp.exp2(grad_ref[i, last : last + 1, :]) for i in range(2 * blocks)]
    for e in range(OWN):
        cuts = sorted({*range(0, capacity + 1, rows), *((share,) if e == 1 else ())})
        pieces = []
        for low, high in zip(cuts, cuts[1:]):
            half = {0: 0, OWN - 1: 1}.get(e, int(low >= share))
            top = low if e != 1 else capacity + low - half * share
            pieces.append((low, high, half, top))
        for low, high, half, top in pieces:
            score = jnp.zeros((high - low, LANE), F32)
            for b in range(blocks):
                at = slice(b * LANE, (b + 1) * LANE)
                grad = grad_ref[2 * b + half, top : top + high - low, :] * scales[2 * b + half]
                by_up = grad * up_factor_ref[e, low:high, at]
                score = score + by_up * up_ref[e, low:high, at].astype(F32)
                up_grad[e, low:high, at] = by_up.astype(BF16)
                gate_grad[e, low:high, at] = (grad * gate_factor_ref[e, low:high, at]).astype(BF16)
            sums = jnp.sum(score, axis=1, keepdims=True)
            near = sums.astype(BF16).astype(F32)
            lane = lax.broadcasted_iota(jnp.int32, (high - low, 2 * LANE - width), 1)
            ends = jnp.where(lane == 0, near, jnp.where(lane == 1, sums - near, 0.0)).astype(BF16)
            group, inner = divmod(low, rows)
            first = (group * OWN + e) * 2 * rows + rows + inner
            back[first : first + high - low, width - LANE :] = ends
        total = dot_nt(gate_grad[e], wg_ref[e]) + dot_nt(up_grad[e], wu_ref[e])
        weight = rows_ref[e, 0:capacity, LANE:].astype(F32)[:, width - LANE : width - LANE + 1]
        total = (total * weight).astype(BF16)
        for group in range(sources // GROUP):
            first = (group * OWN + e) * 2 * rows
            piece = total[group * rows : (group + 1) * rows]
            back[first : first + rows, :] = piece[:, 0:LANE]
            back[first + rows : first + 2 * rows, 0 : width - LANE] = piece[:, LANE:width]
    for g in range(sources // GROUP):
        piece = dot(select_ref[...], back[g * 2 * OWN * rows : (g + 1) * 2 * OWN * rows, :])
        out_ref[g * columns : (g + 1) * columns, :] = piece.astype(BF16)


def combine_kernel(routes_ref, masks_ref, pick_ref, got_ref, tokens_ref, probs_ref, both):
    width, tokens = tokens_ref.shape
    experts = pick_ref.shape[1]
    sums = dot(masks_ref[...], got_ref[...])
    tokens_ref[0:LANE, :] = sums[0:tokens].T
    tokens_ref[LANE:width, :] = sums[tokens:].T[: width - LANE]
    at = lax.broadcasted_iota(jnp.int32, (16, LANE), 1) - lax.broadcasted_iota(jnp.int32, (16, LANE), 0)
    ends = dot_nt((at == width - LANE).astype(F32).astype(BF16), got_ref[...])
    second = masks_ref[tokens:, :].astype(F32)
    both[0:tokens] = (second * ends[0:1, :]).astype(BF16)
    both[tokens:] = (second * ends[1:2, :]).astype(BF16)
    table = dot(both[...], pick_ref[...])
    table = table[0:tokens] + table[tokens:]
    routes = routes_ref[...].astype(F32).T.astype(jnp.int32)
    top = routes.shape[1]
    lane = lax.broadcasted_iota(jnp.int32, (tokens, experts), 1)
    at = lax.broadcasted_iota(jnp.int32, (tokens, top), 1)
    result = jnp.zeros((tokens, top), F32)
    for k in range(top):
        mine = jnp.sum(jnp.where(routes[:, k : k + 1] == lane, table, 0.0), axis=1, keepdims=True)
        result = jnp.where(at == k, mine, result)
    probs_ref[...] = result.T


def cost(flops, nbytes):
    return pl.CostEstimate(flops=flops, bytes_accessed=nbytes, transcendentals=0)


def on_device(cotangent, probs, routes, gate_pre, up_pre, w_gate, w_up, w_down):
    tokens, width = cotangent.shape
    hidden = w_gate.shape[2]
    homes = lax.axis_size("x") * lax.axis_size("z")
    ring = lax.axis_size("y")
    capacity = homes * MOST
    share = -(-capacity // 32) * 16
    blocks = hidden // LANE
    packed = homes * PAIR
    here = lax.axis_index("core").astype(jnp.int32)[None]
    half_shape = jax.ShapeDtypeStruct((blocks, capacity + share, LANE), BF16)
    rows_shape = jax.ShapeDtypeStruct((OWN, 2 * share, 2 * LANE), BF16)

    with jax.named_scope("send_rows"):
        send = pl.pallas_call(
            functools.partial(send_kernel, homes),
            out_shape=jax.ShapeDtypeStruct((packed, LANE), BF16),
            in_specs=[HBM] * 3,
            out_specs=HBM,
            scratch_shapes=[
                pltpu.VMEM((LANE, 3 * tokens), BF16),
                pltpu.VMEM(routes.shape[::-1], jnp.int32),
                pltpu.VMEM(probs.shape[::-1], F32),
                pltpu.VMEM((width, tokens), F32),
                pltpu.VMEM((packed, LANE), BF16),
                pltpu.SemaphoreType.DMA((3,)),
                pltpu.SemaphoreType.DMA((homes // 8,)),
            ],
            compiler_params=WIDE,
            cost_estimate=cost(10**9, 10**6),
        )(routes.T, probs.T, cotangent.T)
    row = np.arange(packed) % PAIR
    place = row % SLOTS
    slot = np.where(place < OWN * MOST, place % MOST, 99)
    slots = np.stack([np.where(row < SLOTS, slot, 99), np.where(row < SLOTS, 99, slot)]).astype(np.float32)
    with jax.named_scope("prepare"):
        factor = jax.ShapeDtypeStruct(gate_pre.shape, F32)
        there, column = 2 * OWN * GROUP * MOST, GROUP * PAIR
        ready = pl.pallas_call(
            functools.partial(prepare_kernel, homes),
            out_shape=(
                factor,
                factor,
                jax.ShapeDtypeStruct((column, there), BF16),
                jax.ShapeDtypeStruct((2 * tokens, packed), BF16),
                jax.ShapeDtypeStruct((packed, homes * OWN), BF16),
            ),
            in_specs=[VMEM] * 4,
            out_specs=(VMEM,) * 5,
            compiler_params=PARAMS,
            cost_estimate=pl.CostEstimate(flops=2 * 10**7, bytes_accessed=2 * 10**7, transcendentals=10**6),
        )(routes.T, jnp.asarray(slots), gate_pre, up_pre)
    with jax.named_scope("dispatch"):
        got = lax.all_to_all(send.reshape(homes, PAIR, LANE), ("x", "z"), 0, 0, tiled=True).reshape(packed, LANE)
        got, (up_factor, gate_factor, select_out, masks, pick) = lax.optimization_barrier((got, ready))
    with jax.named_scope("down_other"):
        rows, other = pl.pallas_call(
            functools.partial(unpack_kernel, share),
            out_shape=(rows_shape, half_shape),
            in_specs=[SMEM, VMEM, VMEM],
            out_specs=(VMEM, VMEM),
            compiler_params=PARAMS,
            cost_estimate=cost(10**9, 4 * 10**6),
        )(here, got, w_down)
    with jax.named_scope("swap_cores"):
        swapped = lax.ppermute(other, "core", [(0, 1), (1, 0)])
    with jax.named_scope("down_own"):
        chip = pl.pallas_call(
            functools.partial(down_kernel, share),
            out_shape=half_shape,
            in_specs=[SMEM, VMEM, VMEM, VMEM],
            out_specs=VMEM,
            compiler_params=PARAMS,
            cost_estimate=cost(10**9, 4 * 10**6),
        )(here, rows, w_down, swapped)
    with jax.named_scope("sum_over_y"):
        parts = lax.all_to_all(chip, "y", 0, 0, tiled=True)
        scaled = pl.pallas_call(
            sum_kernel,
            out_shape=jax.ShapeDtypeStruct((capacity + share + 16, LANE), F32),
            in_specs=[VMEM],
            out_specs=VMEM,
            compiler_params=PARAMS,
            cost_estimate=cost(10**6, 3 * 10**6),
        )(parts)
    with jax.named_scope("gather_hidden"):
        grad = lax.all_gather(scaled.astype(jnp.float16), ("y", "core"), axis=0).astype(F32)
    with jax.named_scope("back"):
        back = pl.pallas_call(
            functools.partial(back_kernel, share),
            out_shape=jax.ShapeDtypeStruct((packed, LANE), BF16),
            in_specs=[VMEM] * 8,
            out_specs=VMEM,
            scratch_shapes=[
                pltpu.VMEM((OWN, capacity, hidden), BF16),
                pltpu.VMEM((OWN, capacity, hidden), BF16),
                pltpu.VMEM((homes * MOST * 2 * OWN, LANE), BF16),
            ],
            compiler_params=PARAMS,
            cost_estimate=cost(2 * 10**9, 10**7),
        )(grad, rows, up_pre, up_factor, gate_factor, w_gate, w_up, select_out)
    with jax.named_scope("way_back"):
        home = lax.all_to_all(back.reshape(homes, PAIR, LANE), ("x", "z"), 0, 0, tiled=True).reshape(packed, LANE)
    with jax.named_scope("combine"):
        grad_tokens, grad_probs = pl.pallas_call(
            combine_kernel,
            out_shape=(
                jax.ShapeDtypeStruct((width, tokens), F32),
                jax.ShapeDtypeStruct(probs.shape[::-1], F32),
            ),
            in_specs=[VMEM] * 4,
            out_specs=(VMEM, VMEM),
            scratch_shapes=[pltpu.VMEM((2 * tokens, packed), BF16)],
            compiler_params=PARAMS,
            cost_estimate=cost(10**9, 10**6),
        )(routes.T, masks, pick, home)
        return grad_tokens.T, grad_probs.T


def solution(mesh):
    node, local = ("y", "core"), ("x", "z")
    y, x = mesh.devices.shape[0] // 2, 4
    parts = Mesh(mesh.devices.reshape(y, 2, x, -1), node + local)
    return jax.shard_map(
        on_device,
        mesh=parts,
        in_specs=(
            P(local, node),
            P(local, None),
            P(local, None),
            P(local, None, None),
            P(local, None, None),
            P(local, node, None),
            P(local, node, None),
            P(local, node, None),
        ),
        out_specs=(P(local, node), P(local, None)),
        check_vma=False,
    )
```

```python
import functools

import jax
import jax.numpy as jnp
import numpy as np
from jax import lax
from jax.experimental import pallas as pl
from jax.experimental.pallas import tpu as pltpu
from jax.sharding import Mesh, PartitionSpec as P

MOST = 9
OWN = 3
SLOTS = 28
PAIR = 2 * SLOTS
LANE = 128
GROUP = 16
F32 = jnp.float32
BF16 = jnp.bfloat16
NT = (((1,), (1,)), ((), ()))
VMEM = pl.BlockSpec(memory_space=pltpu.VMEM)
HBM = pl.BlockSpec(memory_space=pltpu.HBM)
SMEM = pl.BlockSpec(memory_space=pltpu.SMEM)
WIDE = pltpu.CompilerParams(vmem_limit_bytes=62 * 1024 * 1024)
PARAMS = pltpu.CompilerParams(vmem_limit_bytes=24 * 1024 * 1024)


def dot(a, b):
    return jnp.dot(a, b, preferred_element_type=F32)


def dot_nt(a, b):
    return lax.dot_general(a, b, NT, preferred_element_type=F32)


def decode(row):
    second = (row >= SLOTS).astype(jnp.int32)
    place = row - SLOTS * second
    expert = (place >= MOST).astype(jnp.int32) + (place >= 2 * MOST).astype(jnp.int32)
    expert = jnp.minimum(expert, OWN - 1)
    return second, expert, place - MOST * expert


def rank_table(routes, experts):
    tokens, top = routes.shape
    lane = lax.broadcasted_iota(jnp.int32, (tokens, experts), 1)
    hits = [routes[:, k : k + 1] == lane for k in range(top)]
    named = sum(hit.astype(F32) for hit in hits)
    square = (tokens, tokens)
    earlier = lax.broadcasted_iota(jnp.int32, square, 0) > lax.broadcasted_iota(jnp.int32, square, 1)
    rank = dot(earlier.astype(F32).astype(BF16), named.astype(BF16))
    return hits, jnp.where(named > 0.0, rank, 31.0).astype(BF16)


def expert_rows(first, homes, experts):
    shape = (homes, PAIR, experts)
    _, expert, _ = decode(lax.broadcasted_iota(jnp.int32, shape, 1))
    wanted = (lax.broadcasted_iota(jnp.int32, shape, 0) + first) * OWN + expert
    return (lax.broadcasted_iota(jnp.int32, shape, 2) == wanted).reshape(homes * PAIR, experts)


def send_kernel(
    homes, routes_in, probs_in, cot_in, out_hbm, right, routes_ref, probs_ref, cot_ref, out_ref, in_sems, out_sems
):
    width, tokens = cot_ref.shape
    arriving = [
        pltpu.make_async_copy(a, b, in_sems.at[i])
        for i, (a, b) in enumerate(((routes_in, routes_ref), (probs_in, probs_ref), (cot_in, cot_ref)))
    ]
    for copy in arriving:
        copy.start()
    right[...] = jnp.zeros_like(right)
    for copy in arriving:
        copy.wait()
    experts = homes * OWN
    routes = routes_ref[...].astype(F32).T.astype(jnp.int32)
    hits, ranks = rank_table(routes, experts)
    probs = probs_ref[...].T
    weight = sum(jnp.where(hit, probs[:, k : k + 1], 0.0) for k, hit in enumerate(hits)).astype(BF16)
    right[:, 0:tokens] = cot_ref[0:LANE, :].astype(BF16)
    right[0 : width - LANE, tokens : 2 * tokens] = cot_ref[LANE:width, :].astype(BF16)
    mark = lax.broadcasted_iota(jnp.int32, (LANE, tokens), 0) == width - LANE
    right[:, 2 * tokens : 3 * tokens] = mark.astype(F32).astype(BF16)
    step = 8
    leaving = []
    for first in range(0, homes, step):
        pick = expert_rows(first, step, experts).astype(F32).astype(BF16)
        rank_of = dot_nt(pick, ranks)
        weight_of = dot_nt(pick, weight)
        shape = (step, PAIR, tokens)
        second, _, slot = decode(lax.broadcasted_iota(jnp.int32, shape, 1))
        second = second.reshape(step * PAIR, tokens) > 0
        here = rank_of == slot.astype(F32).reshape(step * PAIR, tokens)
        left = jnp.concatenate(
            [
                jnp.where(here & ~second, 1.0, 0.0).astype(BF16),
                jnp.where(here & second, 1.0, 0.0).astype(BF16),
                jnp.where(here & second, weight_of, 0.0).astype(BF16),
            ],
            axis=1,
        )
        there = slice(first * PAIR, (first + step) * PAIR)
        out_ref[there, :] = dot_nt(left, right[...]).astype(BF16)
        leaving.append(pltpu.make_async_copy(out_ref.at[there], out_hbm.at[there], out_sems.at[first // step]))
        leaving[-1].start()
    for copy in leaving:
        copy.wait()


def down_half(half, share, rows_ref, w_ref, out_ref, plus_ref=None, here=None):
    capacity = out_ref.shape[1] - share
    whole = half * (OWN - 1)
    width, hidden = w_ref.shape[1:]
    left = rows_ref[whole, 0:capacity, 0:width]
    part = rows_ref[1, pl.ds(pl.multiple_of(half * share, 16), share), 0:width]
    tile = 2 * LANE
    for n in range(hidden // tile):
        columns = slice(n * tile, (n + 1) * tile)
        for a, top, count in (
            (dot(left, w_ref[whole, :, columns]), 0, capacity),
            (dot(part, w_ref[1, :, columns]), capacity, share),
        ):
            for m, piece in ((2 * n, a[:, :LANE]), (2 * n + 1, a[:, LANE:])):
                if plus_ref is not None:
                    piece = piece + plus_ref[m, top : top + count, :].astype(F32)
                at = m if here is None else lax.rem(m + out_ref.shape[0] - here, out_ref.shape[0])
                out_ref[at, top : top + count, :] = piece.astype(BF16)


def unpack_kernel(share, half_ref, got_ref, w_ref, rows_ref, out_ref):
    sources = got_ref.shape[0] // PAIR
    capacity = sources * MOST
    rows, columns = GROUP * MOST, GROUP * PAIR
    at = lax.broadcasted_iota(jnp.int32, (1, columns), 1)
    source = jnp.floor((at.astype(F32) + 0.5) * (1.0 / PAIR)).astype(jnp.int32)
    second, expert, slot = decode(at - PAIR * source)
    goal = jnp.where(slot < MOST, (2 * expert + second) * rows + source * MOST + slot, -1)
    select = lax.broadcasted_iota(jnp.int32, (2 * OWN * rows, columns), 0) == goal
    select = select.astype(F32).astype(BF16)
    rows_ref[:, capacity:, :] = jnp.zeros((OWN, rows_ref.shape[1] - capacity, 2 * LANE), BF16)
    for g in range(sources // GROUP):
        piece = dot(select, got_ref[g * columns : (g + 1) * columns, :]).astype(BF16)
        for e in range(OWN):
            for second in range(2):
                top = (2 * e + second) * rows
                rows_ref[e, g * rows : (g + 1) * rows, second * LANE : (second + 1) * LANE] = piece[top : top + rows]
    down_half(1 - half_ref[0], share, rows_ref, w_ref, out_ref)


def down_kernel(share, half_ref, rows_ref, w_ref, plus_ref, own_ref, right_ref, left_ref, right_far_ref, left_far_ref, ring):
    down_half(half_ref[0], share, rows_ref, w_ref, ring, plus_ref, half_ref[1])
    for out, distances in ((own_ref, (0, 2, 6)), (right_ref, (1, 3)), (left_ref, (7, 5))):
        for i, k in enumerate(distances):
            out[i] = ring[k]
    near = right_far_ref.shape[0]
    right_far_ref[...] = ring[4, 0:near, :]
    left_far_ref[...] = ring[4, near:, :]


def relay_kernel(own_ref, right_ref, left_ref, right_far_ref, left_far_ref, right_out, left_out):
    near = right_far_ref.shape[0]
    right = own_ref[1].astype(F32) + right_ref[1].astype(F32)
    left = own_ref[2].astype(F32) + left_ref[1].astype(F32)
    right_out[0:near, :] = (right[0:near] + right_far_ref[...].astype(F32)).astype(BF16)
    right_out[near:, :] = right[near:].astype(BF16)
    left_out[0:near, :] = left[0:near].astype(BF16)
    left_out[near:, :] = (left[near:] + left_far_ref[...].astype(F32)).astype(BF16)


def prepare_kernel(
    homes, routes_ref, slots_ref, gate_ref, up_ref,
    up_factor_ref, gate_factor_ref, select_out_ref, masks_ref, pick_ref,
):
    capacity, hidden = gate_ref.shape[1:]
    experts = homes * OWN
    step = 48
    for e in range(OWN):

        def part(i, carry, e=e):
            rows = pl.ds(pl.multiple_of(i * step, step), step)
            for b in range(0, hidden, LANE):
                gate = gate_ref[e, rows, b : b + LANE].astype(F32)
                up = up_ref[e, rows, b : b + LANE].astype(F32)
                sig = lax.logistic(gate)
                up_factor_ref[e, rows, b : b + LANE] = gate * sig
                gate_factor_ref[e, rows, b : b + LANE] = up * sig * (1.0 + gate * (1.0 - sig))
            return carry

        lax.fori_loop(0, capacity // step, part, 0)
    rows, columns = GROUP * MOST, GROUP * PAIR
    shape = (GROUP, PAIR, 2 * OWN * rows)
    second, expert, slot = decode(lax.broadcasted_iota(jnp.int32, shape, 1))
    goal = (2 * expert + second) * rows + lax.broadcasted_iota(jnp.int32, shape, 0) * MOST + slot
    select = (lax.broadcasted_iota(jnp.int32, shape, 2) == goal) & (slot < MOST)
    select_out_ref[...] = select.reshape(columns, 2 * OWN * rows).astype(F32).astype(BF16)
    _, ranks = rank_table(routes_ref[...].astype(F32).T.astype(jnp.int32), experts)
    pick_ref[...] = expert_rows(0, homes, experts).astype(F32).astype(BF16)
    rank_of = dot_nt(ranks, pick_ref[...])
    tokens = rank_of.shape[0]
    masks_ref[0:tokens] = (rank_of == slots_ref[0:1, :]).astype(F32).astype(BF16)
    masks_ref[tokens:] = (rank_of == slots_ref[1:2, :]).astype(F32).astype(BF16)


def sum_kernel(own_ref, right_ref, left_ref, right_two_ref, left_two_ref, out_ref):
    rows = own_ref.shape[1]
    total = own_ref[0].astype(F32) + right_ref[0].astype(F32) + left_ref[0].astype(F32)
    total = total + right_two_ref[...].astype(F32) + left_two_ref[...].astype(F32)
    largest = jnp.max(jnp.max(jnp.abs(total), axis=0, keepdims=True), axis=1, keepdims=True)
    largest = jnp.broadcast_to(jnp.maximum(largest, 1e-35), (16, LANE))
    power = jnp.clip(jnp.floor(jnp.log2(largest)), -100.0, 100.0)
    out_ref[0:rows, :] = total * jnp.exp2(-power)[0:1]
    out_ref[rows:, :] = power


def back_kernel(
    share, grad_ref, rows_ref, up_ref, up_factor_ref, gate_factor_ref, wg_ref, wu_ref, select_ref, out_ref,
    gate_grad, up_grad, back,
):
    sources = out_ref.shape[0] // PAIR
    capacity = sources * MOST
    width = wg_ref.shape[1]
    blocks = up_ref.shape[2] // LANE
    rows, columns = GROUP * MOST, GROUP * PAIR
    last = capacity + share
    scales = [jnp.exp2(grad_ref[i, last : last + 1, :]) for i in range(2 * blocks)]
    for e in range(OWN):
        cuts = sorted({*range(0, capacity + 1, rows), *((share,) if e == 1 else ())})
        pieces = []
        for low, high in zip(cuts, cuts[1:]):
            half = {0: 0, OWN - 1: 1}.get(e, int(low >= share))
            top = low if e != 1 else capacity + low - half * share
            pieces.append((low, high, half, top))
        for low, high, half, top in pieces:
            score = jnp.zeros((high - low, LANE), F32)
            for b in range(blocks):
                at = slice(b * LANE, (b + 1) * LANE)
                grad = grad_ref[2 * b + half, top : top + high - low, :] * scales[2 * b + half]
                by_up = grad * up_factor_ref[e, low:high, at]
                score = score + by_up * up_ref[e, low:high, at].astype(F32)
                up_grad[e, low:high, at] = by_up.astype(BF16)
                gate_grad[e, low:high, at] = (grad * gate_factor_ref[e, low:high, at]).astype(BF16)
            sums = jnp.sum(score, axis=1, keepdims=True)
            near = sums.astype(BF16).astype(F32)
            lane = lax.broadcasted_iota(jnp.int32, (high - low, 2 * LANE - width), 1)
            ends = jnp.where(lane == 0, near, jnp.where(lane == 1, sums - near, 0.0)).astype(BF16)
            group, inner = divmod(low, rows)
            first = (group * OWN + e) * 2 * rows + rows + inner
            back[first : first + high - low, width - LANE :] = ends
        total = dot_nt(gate_grad[e], wg_ref[e]) + dot_nt(up_grad[e], wu_ref[e])
        weight = rows_ref[e, 0:capacity, LANE:].astype(F32)[:, width - LANE : width - LANE + 1]
        total = (total * weight).astype(BF16)
        for group in range(sources // GROUP):
            first = (group * OWN + e) * 2 * rows
            piece = total[group * rows : (group + 1) * rows]
            back[first : first + rows, :] = piece[:, 0:LANE]
            back[first + rows : first + 2 * rows, 0 : width - LANE] = piece[:, LANE:width]
    for g in range(sources // GROUP):
        piece = dot(select_ref[...], back[g * 2 * OWN * rows : (g + 1) * 2 * OWN * rows, :])
        out_ref[g * columns : (g + 1) * columns, :] = piece.astype(BF16)


def combine_kernel(routes_ref, masks_ref, pick_ref, got_ref, tokens_ref, probs_ref, both):
    width, tokens = tokens_ref.shape
    experts = pick_ref.shape[1]
    sums = dot(masks_ref[...], got_ref[...])
    tokens_ref[0:LANE, :] = sums[0:tokens].T
    tokens_ref[LANE:width, :] = sums[tokens:].T[: width - LANE]
    at = lax.broadcasted_iota(jnp.int32, (16, LANE), 1) - lax.broadcasted_iota(jnp.int32, (16, LANE), 0)
    ends = dot_nt((at == width - LANE).astype(F32).astype(BF16), got_ref[...])
    second = masks_ref[tokens:, :].astype(F32)
    both[0:tokens] = (second * ends[0:1, :]).astype(BF16)
    both[tokens:] = (second * ends[1:2, :]).astype(BF16)
    table = dot(both[...], pick_ref[...])
    table = table[0:tokens] + table[tokens:]
    routes = routes_ref[...].astype(F32).T.astype(jnp.int32)
    top = routes.shape[1]
    lane = lax.broadcasted_iota(jnp.int32, (tokens, experts), 1)
    at = lax.broadcasted_iota(jnp.int32, (tokens, top), 1)
    result = jnp.zeros((tokens, top), F32)
    for k in range(top):
        mine = jnp.sum(jnp.where(routes[:, k : k + 1] == lane, table, 0.0), axis=1, keepdims=True)
        result = jnp.where(at == k, mine, result)
    probs_ref[...] = result.T


def cost(flops, nbytes):
    return pl.CostEstimate(flops=flops, bytes_accessed=nbytes, transcendentals=0)


def on_device(cotangent, probs, routes, gate_pre, up_pre, w_gate, w_up, w_down):
    tokens, width = cotangent.shape
    hidden = w_gate.shape[2]
    homes = lax.axis_size("x") * lax.axis_size("z")
    ring = lax.axis_size("y")
    capacity = homes * MOST
    share = -(-capacity // 32) * 16
    blocks = hidden // LANE
    packed = homes * PAIR
    here = jnp.stack([lax.axis_index("core"), lax.axis_index("y")]).astype(jnp.int32)
    half_shape = jax.ShapeDtypeStruct((blocks, capacity + share, LANE), BF16)
    rows_shape = jax.ShapeDtypeStruct((OWN, 2 * share, 2 * LANE), BF16)

    with jax.named_scope("send_rows"):
        send = pl.pallas_call(
            functools.partial(send_kernel, homes),
            out_shape=jax.ShapeDtypeStruct((packed, LANE), BF16),
            in_specs=[HBM] * 3,
            out_specs=HBM,
            scratch_shapes=[
                pltpu.VMEM((LANE, 3 * tokens), BF16),
                pltpu.VMEM(routes.shape[::-1], jnp.int32),
                pltpu.VMEM(probs.shape[::-1], F32),
                pltpu.VMEM((width, tokens), F32),
                pltpu.VMEM((packed, LANE), BF16),
                pltpu.SemaphoreType.DMA((3,)),
                pltpu.SemaphoreType.DMA((homes // 8,)),
            ],
            compiler_params=WIDE,
            cost_estimate=cost(10**9, 10**6),
        )(routes.T, probs.T, cotangent.T)
    row = np.arange(packed) % PAIR
    place = row % SLOTS
    slot = np.where(place < OWN * MOST, place % MOST, 99)
    slots = np.stack([np.where(row < SLOTS, slot, 99), np.where(row < SLOTS, 99, slot)]).astype(np.float32)
    with jax.named_scope("prepare"):
        factor = jax.ShapeDtypeStruct(gate_pre.shape, F32)
        there, column = 2 * OWN * GROUP * MOST, GROUP * PAIR
        ready = pl.pallas_call(
            functools.partial(prepare_kernel, homes),
            out_shape=(
                factor,
                factor,
                jax.ShapeDtypeStruct((column, there), BF16),
                jax.ShapeDtypeStruct((2 * tokens, packed), BF16),
                jax.ShapeDtypeStruct((packed, homes * OWN), BF16),
            ),
            in_specs=[VMEM] * 4,
            out_specs=(VMEM,) * 5,
            compiler_params=PARAMS,
            cost_estimate=pl.CostEstimate(flops=2 * 10**7, bytes_accessed=2 * 10**7, transcendentals=10**6),
        )(routes.T, jnp.asarray(slots), gate_pre, up_pre)
    with jax.named_scope("dispatch"):
        got = lax.all_to_all(send.reshape(homes, PAIR, LANE), ("x", "z"), 0, 0, tiled=True).reshape(packed, LANE)
        got, (up_factor, gate_factor, select_out, masks, pick) = lax.optimization_barrier((got, ready))
    with jax.named_scope("down_other"):
        rows, other = pl.pallas_call(
            functools.partial(unpack_kernel, share),
            out_shape=(rows_shape, half_shape),
            in_specs=[SMEM, VMEM, VMEM],
            out_specs=(VMEM, VMEM),
            compiler_params=PARAMS,
            cost_estimate=cost(10**9, 4 * 10**6),
        )(here, got, w_down)
    with jax.named_scope("swap_cores"):
        swapped = lax.ppermute(other, "core", [(0, 1), (1, 0)])
    with jax.named_scope("down_own"):
        tall = capacity + share
        near = -(-tall // 32) * 16
        own, right, left, right_far, left_far = pl.pallas_call(
            functools.partial(down_kernel, share),
            out_shape=[
                jax.ShapeDtypeStruct(shape, BF16)
                for shape in ((3, tall, LANE), (2, tall, LANE), (2, tall, LANE), (near, LANE), (tall - near, LANE))
            ],
            in_specs=[SMEM, VMEM, VMEM, VMEM],
            out_specs=[VMEM] * 5,
            scratch_shapes=[pltpu.VMEM(half_shape.shape, BF16)],
            compiler_params=PARAMS,
            cost_estimate=cost(10**9, 4 * 10**6),
        )(here, rows, w_down, swapped)
    with jax.named_scope("sum_over_y"):
        def shifted(value, by):
            return lax.ppermute(value, "y", [(i, (i + by) % blocks) for i in range(blocks)])

        right, left = shifted(right, 1), shifted(left, -1)
        right_far, left_far = shifted(right_far, 2), shifted(left_far, -2)
        right_two, left_two = pl.pallas_call(
            relay_kernel,
            out_shape=[jax.ShapeDtypeStruct((tall, LANE), BF16)] * 2,
            in_specs=[VMEM] * 5,
            out_specs=[VMEM] * 2,
            compiler_params=PARAMS,
            cost_estimate=cost(10**6, 2 * 10**6),
        )(own, right, left, right_far, left_far)
        right_two, left_two = shifted(right_two, 2), shifted(left_two, -2)
        scaled = pl.pallas_call(
            sum_kernel,
            out_shape=jax.ShapeDtypeStruct((capacity + share + 16, LANE), F32),
            in_specs=[VMEM] * 5,
            out_specs=VMEM,
            compiler_params=PARAMS,
            cost_estimate=cost(10**6, 3 * 10**6),
        )(own, right, left, right_two, left_two)
    with jax.named_scope("gather_hidden"):
        grad = lax.all_gather(scaled.astype(jnp.float16), ("y", "core"), axis=0).astype(F32)
    with jax.named_scope("back"):
        back = pl.pallas_call(
            functools.partial(back_kernel, share),
            out_shape=jax.ShapeDtypeStruct((packed, LANE), BF16),
            in_specs=[VMEM] * 8,
            out_specs=VMEM,
            scratch_shapes=[
                pltpu.VMEM((OWN, capacity, hidden), BF16),
                pltpu.VMEM((OWN, capacity, hidden), BF16),
                pltpu.VMEM((homes * MOST * 2 * OWN, LANE), BF16),
            ],
            compiler_params=PARAMS,
            cost_estimate=cost(2 * 10**9, 10**7),
        )(grad, rows, up_pre, up_factor, gate_factor, w_gate, w_up, select_out)
    with jax.named_scope("way_back"):
        home = lax.all_to_all(back.reshape(homes, PAIR, LANE), ("x", "z"), 0, 0, tiled=True).reshape(packed, LANE)
    with jax.named_scope("combine"):
        grad_tokens, grad_probs = pl.pallas_call(
            combine_kernel,
            out_shape=(
                jax.ShapeDtypeStruct((width, tokens), F32),
                jax.ShapeDtypeStruct(probs.shape[::-1], F32),
            ),
            in_specs=[VMEM] * 4,
            out_specs=(VMEM, VMEM),
            scratch_shapes=[pltpu.VMEM((2 * tokens, packed), BF16)],
            compiler_params=PARAMS,
            cost_estimate=cost(10**9, 10**6),
        )(routes.T, masks, pick, home)
        return grad_tokens.T, grad_probs.T


def solution(mesh):
    node, local = ("y", "core"), ("x", "z")
    y, x = mesh.devices.shape[0] // 2, 4
    parts = Mesh(mesh.devices.reshape(y, 2, x, -1), node + local)
    return jax.shard_map(
        on_device,
        mesh=parts,
        in_specs=(
            P(local, node),
            P(local, None),
            P(local, None),
            P(local, None, None),
            P(local, None, None),
            P(local, node, None),
            P(local, node, None),
            P(local, node, None),
        ),
        out_specs=(P(local, node), P(local, None)),
        check_vma=False,
    )
```

```python
import functools

import jax
import jax.numpy as jnp
import numpy as np
from jax import lax
from jax.experimental import pallas as pl
from jax.experimental.pallas import tpu as pltpu
from jax.sharding import Mesh, PartitionSpec as P

MOST = 9
OWN = 3
SLOTS = 28
PAIR = 2 * SLOTS
LANE = 128
GROUP = 16
F32 = jnp.float32
BF16 = jnp.bfloat16
NT = (((1,), (1,)), ((), ()))
VMEM = pl.BlockSpec(memory_space=pltpu.VMEM)
HBM = pl.BlockSpec(memory_space=pltpu.HBM)
SMEM = pl.BlockSpec(memory_space=pltpu.SMEM)
WIDE = pltpu.CompilerParams(vmem_limit_bytes=62 * 1024 * 1024)
PARAMS = pltpu.CompilerParams(vmem_limit_bytes=24 * 1024 * 1024)


def dot(a, b):
    return jnp.dot(a, b, preferred_element_type=F32)


def dot_nt(a, b):
    return lax.dot_general(a, b, NT, preferred_element_type=F32)


def decode(row):
    second = (row >= SLOTS).astype(jnp.int32)
    place = row - SLOTS * second
    expert = (place >= MOST).astype(jnp.int32) + (place >= 2 * MOST).astype(jnp.int32)
    expert = jnp.minimum(expert, OWN - 1)
    return second, expert, place - MOST * expert


def rank_table(routes, experts):
    tokens, top = routes.shape
    lane = lax.broadcasted_iota(jnp.int32, (tokens, experts), 1)
    hits = [routes[:, k : k + 1] == lane for k in range(top)]
    named = sum(hit.astype(F32) for hit in hits)
    square = (tokens, tokens)
    earlier = lax.broadcasted_iota(jnp.int32, square, 0) > lax.broadcasted_iota(jnp.int32, square, 1)
    rank = dot(earlier.astype(F32).astype(BF16), named.astype(BF16))
    return hits, jnp.where(named > 0.0, rank, 31.0).astype(BF16)


def expert_rows(first, homes, experts):
    shape = (homes, PAIR, experts)
    _, expert, _ = decode(lax.broadcasted_iota(jnp.int32, shape, 1))
    wanted = (lax.broadcasted_iota(jnp.int32, shape, 0) + first) * OWN + expert
    return (lax.broadcasted_iota(jnp.int32, shape, 2) == wanted).reshape(homes * PAIR, experts)


def send_kernel(
    homes, routes_in, probs_in, cot_in, out_hbm, right, routes_ref, probs_ref, cot_ref, out_ref, in_sems, out_sems
):
    width, tokens = cot_ref.shape
    arriving = [
        pltpu.make_async_copy(a, b, in_sems.at[i])
        for i, (a, b) in enumerate(((routes_in, routes_ref), (probs_in, probs_ref), (cot_in, cot_ref)))
    ]
    for copy in arriving:
        copy.start()
    right[...] = jnp.zeros_like(right)
    for copy in arriving:
        copy.wait()
    experts = homes * OWN
    routes = routes_ref[...].astype(F32).T.astype(jnp.int32)
    hits, ranks = rank_table(routes, experts)
    probs = probs_ref[...].T
    weight = sum(jnp.where(hit, probs[:, k : k + 1], 0.0) for k, hit in enumerate(hits)).astype(BF16)
    right[:, 0:tokens] = cot_ref[0:LANE, :].astype(BF16)
    right[0 : width - LANE, tokens : 2 * tokens] = cot_ref[LANE:width, :].astype(BF16)
    mark = lax.broadcasted_iota(jnp.int32, (LANE, tokens), 0) == width - LANE
    right[:, 2 * tokens : 3 * tokens] = mark.astype(F32).astype(BF16)
    step = 8
    leaving = []
    for first in range(0, homes, step):
        pick = expert_rows(first, step, experts).astype(F32).astype(BF16)
        rank_of = dot_nt(pick, ranks)
        weight_of = dot_nt(pick, weight)
        shape = (step, PAIR, tokens)
        second, _, slot = decode(lax.broadcasted_iota(jnp.int32, shape, 1))
        second = second.reshape(step * PAIR, tokens) > 0
        here = rank_of == slot.astype(F32).reshape(step * PAIR, tokens)
        left = jnp.concatenate(
            [
                jnp.where(here & ~second, 1.0, 0.0).astype(BF16),
                jnp.where(here & second, 1.0, 0.0).astype(BF16),
                jnp.where(here & second, weight_of, 0.0).astype(BF16),
            ],
            axis=1,
        )
        there = slice(first * PAIR, (first + step) * PAIR)
        out_ref[there, :] = dot_nt(left, right[...]).astype(BF16)
        leaving.append(pltpu.make_async_copy(out_ref.at[there], out_hbm.at[there], out_sems.at[first // step]))
        leaving[-1].start()
    for copy in leaving:
        copy.wait()


def down_half(half, share, rows_ref, w_ref, out_ref, plus_ref=None, here=None):
    capacity = out_ref.shape[1] - share
    whole = half * (OWN - 1)
    width, hidden = w_ref.shape[1:]
    left = rows_ref[whole, 0:capacity, 0:width]
    part = rows_ref[1, pl.ds(pl.multiple_of(half * share, 16), share), 0:width]
    tile = 2 * LANE
    for n in range(hidden // tile):
        columns = slice(n * tile, (n + 1) * tile)
        for a, top, count in (
            (dot(left, w_ref[whole, :, columns]), 0, capacity),
            (dot(part, w_ref[1, :, columns]), capacity, share),
        ):
            for m, piece in ((2 * n, a[:, :LANE]), (2 * n + 1, a[:, LANE:])):
                if plus_ref is not None:
                    piece = piece + plus_ref[m, top : top + count, :].astype(F32)
                at = m if here is None else lax.rem(m + out_ref.shape[0] - here, out_ref.shape[0])
                out_ref[at, top : top + count, :] = piece.astype(BF16)


def unpack_kernel(share, half_ref, got_ref, w_ref, rows_ref, out_ref):
    sources = got_ref.shape[0] // PAIR
    capacity = sources * MOST
    rows, columns = GROUP * MOST, GROUP * PAIR
    at = lax.broadcasted_iota(jnp.int32, (1, columns), 1)
    source = jnp.floor((at.astype(F32) + 0.5) * (1.0 / PAIR)).astype(jnp.int32)
    second, expert, slot = decode(at - PAIR * source)
    goal = jnp.where(slot < MOST, (2 * expert + second) * rows + source * MOST + slot, -1)
    select = lax.broadcasted_iota(jnp.int32, (2 * OWN * rows, columns), 0) == goal
    select = select.astype(F32).astype(BF16)
    rows_ref[:, capacity:, :] = jnp.zeros((OWN, rows_ref.shape[1] - capacity, 2 * LANE), BF16)
    for g in range(sources // GROUP):
        piece = dot(select, got_ref[g * columns : (g + 1) * columns, :]).astype(BF16)
        for e in range(OWN):
            for second in range(2):
                top = (2 * e + second) * rows
                rows_ref[e, g * rows : (g + 1) * rows, second * LANE : (second + 1) * LANE] = piece[top : top + rows]
    down_half(1 - half_ref[0], share, rows_ref, w_ref, out_ref)


def down_kernel(share, half_ref, rows_ref, w_ref, plus_ref, own_ref, right_ref, left_ref, far_ref, ring):
    down_half(half_ref[0], share, rows_ref, w_ref, ring, plus_ref, half_ref[1])
    for out, distances in ((own_ref, (0, 2, 6)), (right_ref, (1, 3)), (left_ref, (7, 5))):
        for i, k in enumerate(distances):
            out[i] = ring[k]
    far_ref[...] = ring[4]


def relay_kernel(own_ref, right_ref, left_ref, far_ref, right_out, left_out):
    right = own_ref[1].astype(F32) + right_ref[1].astype(F32) + far_ref[...].astype(F32)
    right_out[...] = right.astype(BF16)
    left_out[...] = (own_ref[2].astype(F32) + left_ref[1].astype(F32)).astype(BF16)


def prepare_kernel(
    homes, routes_ref, slots_ref, gate_ref, up_ref,
    up_factor_ref, gate_factor_ref, select_out_ref, masks_ref, pick_ref,
):
    capacity, hidden = gate_ref.shape[1:]
    experts = homes * OWN
    step = 48
    for e in range(OWN):

        def part(i, carry, e=e):
            rows = pl.ds(pl.multiple_of(i * step, step), step)
            for b in range(0, hidden, LANE):
                gate = gate_ref[e, rows, b : b + LANE].astype(F32)
                up = up_ref[e, rows, b : b + LANE].astype(F32)
                sig = lax.logistic(gate)
                up_factor_ref[e, rows, b : b + LANE] = gate * sig
                gate_factor_ref[e, rows, b : b + LANE] = up * sig * (1.0 + gate * (1.0 - sig))
            return carry

        lax.fori_loop(0, capacity // step, part, 0)
    rows, columns = GROUP * MOST, GROUP * PAIR
    shape = (GROUP, PAIR, 2 * OWN * rows)
    second, expert, slot = decode(lax.broadcasted_iota(jnp.int32, shape, 1))
    goal = (2 * expert + second) * rows + lax.broadcasted_iota(jnp.int32, shape, 0) * MOST + slot
    select = (lax.broadcasted_iota(jnp.int32, shape, 2) == goal) & (slot < MOST)
    select_out_ref[...] = select.reshape(columns, 2 * OWN * rows).astype(F32).astype(BF16)
    _, ranks = rank_table(routes_ref[...].astype(F32).T.astype(jnp.int32), experts)
    pick_ref[...] = expert_rows(0, homes, experts).astype(F32).astype(BF16)
    rank_of = dot_nt(ranks, pick_ref[...])
    tokens = rank_of.shape[0]
    masks_ref[0:tokens] = (rank_of == slots_ref[0:1, :]).astype(F32).astype(BF16)
    masks_ref[tokens:] = (rank_of == slots_ref[1:2, :]).astype(F32).astype(BF16)


def sum_kernel(own_ref, right_ref, left_ref, right_two_ref, left_two_ref, out_ref):
    rows = own_ref.shape[1]
    total = own_ref[0].astype(F32) + right_ref[0].astype(F32) + left_ref[0].astype(F32)
    total = total + right_two_ref[...].astype(F32) + left_two_ref[...].astype(F32)
    largest = jnp.max(jnp.max(jnp.abs(total), axis=0, keepdims=True), axis=1, keepdims=True)
    largest = jnp.broadcast_to(jnp.maximum(largest, 1e-35), (16, LANE))
    power = jnp.clip(jnp.floor(jnp.log2(largest)), -100.0, 100.0)
    out_ref[0:rows, :] = total * jnp.exp2(-power)[0:1]
    out_ref[rows:, :] = power


def back_kernel(
    share, grad_ref, rows_ref, up_ref, up_factor_ref, gate_factor_ref, wg_ref, wu_ref, select_ref, out_ref,
    gate_grad, up_grad, back,
):
    sources = out_ref.shape[0] // PAIR
    capacity = sources * MOST
    width = wg_ref.shape[1]
    blocks = up_ref.shape[2] // LANE
    rows, columns = GROUP * MOST, GROUP * PAIR
    last = capacity + share
    scales = [jnp.exp2(grad_ref[i, last : last + 1, :]) for i in range(2 * blocks)]
    for e in range(OWN):
        cuts = sorted({*range(0, capacity + 1, rows), *((share,) if e == 1 else ())})
        pieces = []
        for low, high in zip(cuts, cuts[1:]):
            half = {0: 0, OWN - 1: 1}.get(e, int(low >= share))
            top = low if e != 1 else capacity + low - half * share
            pieces.append((low, high, half, top))
        for low, high, half, top in pieces:
            score = jnp.zeros((high - low, LANE), F32)
            for b in range(blocks):
                at = slice(b * LANE, (b + 1) * LANE)
                grad = grad_ref[2 * b + half, top : top + high - low, :] * scales[2 * b + half]
                by_up = grad * up_factor_ref[e, low:high, at]
                score = score + by_up * up_ref[e, low:high, at].astype(F32)
                up_grad[e, low:high, at] = by_up.astype(BF16)
                gate_grad[e, low:high, at] = (grad * gate_factor_ref[e, low:high, at]).astype(BF16)
            sums = jnp.sum(score, axis=1, keepdims=True)
            near = sums.astype(BF16).astype(F32)
            lane = lax.broadcasted_iota(jnp.int32, (high - low, 2 * LANE - width), 1)
            ends = jnp.where(lane == 0, near, jnp.where(lane == 1, sums - near, 0.0)).astype(BF16)
            group, inner = divmod(low, rows)
            first = (group * OWN + e) * 2 * rows + rows + inner
            back[first : first + high - low, width - LANE :] = ends
        total = dot_nt(gate_grad[e], wg_ref[e]) + dot_nt(up_grad[e], wu_ref[e])
        weight = rows_ref[e, 0:capacity, LANE:].astype(F32)[:, width - LANE : width - LANE + 1]
        total = (total * weight).astype(BF16)
        for group in range(sources // GROUP):
            first = (group * OWN + e) * 2 * rows
            piece = total[group * rows : (group + 1) * rows]
            back[first : first + rows, :] = piece[:, 0:LANE]
            back[first + rows : first + 2 * rows, 0 : width - LANE] = piece[:, LANE:width]
    for g in range(sources // GROUP):
        piece = dot(select_ref[...], back[g * 2 * OWN * rows : (g + 1) * 2 * OWN * rows, :])
        out_ref[g * columns : (g + 1) * columns, :] = piece.astype(BF16)


def combine_kernel(routes_ref, masks_ref, pick_ref, got_ref, tokens_ref, probs_ref, both):
    width, tokens = tokens_ref.shape
    experts = pick_ref.shape[1]
    sums = dot(masks_ref[...], got_ref[...])
    tokens_ref[0:LANE, :] = sums[0:tokens].T
    tokens_ref[LANE:width, :] = sums[tokens:].T[: width - LANE]
    at = lax.broadcasted_iota(jnp.int32, (16, LANE), 1) - lax.broadcasted_iota(jnp.int32, (16, LANE), 0)
    ends = dot_nt((at == width - LANE).astype(F32).astype(BF16), got_ref[...])
    second = masks_ref[tokens:, :].astype(F32)
    both[0:tokens] = (second * ends[0:1, :]).astype(BF16)
    both[tokens:] = (second * ends[1:2, :]).astype(BF16)
    table = dot(both[...], pick_ref[...])
    table = table[0:tokens] + table[tokens:]
    routes = routes_ref[...].astype(F32).T.astype(jnp.int32)
    top = routes.shape[1]
    lane = lax.broadcasted_iota(jnp.int32, (tokens, experts), 1)
    at = lax.broadcasted_iota(jnp.int32, (tokens, top), 1)
    result = jnp.zeros((tokens, top), F32)
    for k in range(top):
        mine = jnp.sum(jnp.where(routes[:, k : k + 1] == lane, table, 0.0), axis=1, keepdims=True)
        result = jnp.where(at == k, mine, result)
    probs_ref[...] = result.T


def cost(flops, nbytes):
    return pl.CostEstimate(flops=flops, bytes_accessed=nbytes, transcendentals=0)


def on_device(cotangent, probs, routes, gate_pre, up_pre, w_gate, w_up, w_down):
    tokens, width = cotangent.shape
    hidden = w_gate.shape[2]
    homes = lax.axis_size("x") * lax.axis_size("z")
    ring = lax.axis_size("y")
    capacity = homes * MOST
    share = -(-capacity // 32) * 16
    blocks = hidden // LANE
    packed = homes * PAIR
    here = jnp.stack([lax.axis_index("core"), lax.axis_index("y")]).astype(jnp.int32)
    half_shape = jax.ShapeDtypeStruct((blocks, capacity + share, LANE), BF16)
    rows_shape = jax.ShapeDtypeStruct((OWN, 2 * share, 2 * LANE), BF16)

    with jax.named_scope("send_rows"):
        send = pl.pallas_call(
            functools.partial(send_kernel, homes),
            out_shape=jax.ShapeDtypeStruct((packed, LANE), BF16),
            in_specs=[HBM] * 3,
            out_specs=HBM,
            scratch_shapes=[
                pltpu.VMEM((LANE, 3 * tokens), BF16),
                pltpu.VMEM(routes.shape[::-1], jnp.int32),
                pltpu.VMEM(probs.shape[::-1], F32),
                pltpu.VMEM((width, tokens), F32),
                pltpu.VMEM((packed, LANE), BF16),
                pltpu.SemaphoreType.DMA((3,)),
                pltpu.SemaphoreType.DMA((homes // 8,)),
            ],
            compiler_params=WIDE,
            cost_estimate=cost(10**9, 10**6),
        )(routes.T, probs.T, cotangent.T)
    row = np.arange(packed) % PAIR
    place = row % SLOTS
    slot = np.where(place < OWN * MOST, place % MOST, 99)
    slots = np.stack([np.where(row < SLOTS, slot, 99), np.where(row < SLOTS, 99, slot)]).astype(np.float32)
    with jax.named_scope("prepare"):
        factor = jax.ShapeDtypeStruct(gate_pre.shape, F32)
        there, column = 2 * OWN * GROUP * MOST, GROUP * PAIR
        ready = pl.pallas_call(
            functools.partial(prepare_kernel, homes),
            out_shape=(
                factor,
                factor,
                jax.ShapeDtypeStruct((column, there), BF16),
                jax.ShapeDtypeStruct((2 * tokens, packed), BF16),
                jax.ShapeDtypeStruct((packed, homes * OWN), BF16),
            ),
            in_specs=[VMEM] * 4,
            out_specs=(VMEM,) * 5,
            compiler_params=PARAMS,
            cost_estimate=pl.CostEstimate(flops=2 * 10**7, bytes_accessed=2 * 10**7, transcendentals=10**6),
        )(routes.T, jnp.asarray(slots), gate_pre, up_pre)
    with jax.named_scope("dispatch"):
        got = lax.all_to_all(send.reshape(homes, PAIR, LANE), ("x", "z"), 0, 0, tiled=True).reshape(packed, LANE)
        got, (up_factor, gate_factor, select_out, masks, pick) = lax.optimization_barrier((got, ready))
    with jax.named_scope("down_other"):
        rows, other = pl.pallas_call(
            functools.partial(unpack_kernel, share),
            out_shape=(rows_shape, half_shape),
            in_specs=[SMEM, VMEM, VMEM],
            out_specs=(VMEM, VMEM),
            compiler_params=PARAMS,
            cost_estimate=cost(10**9, 4 * 10**6),
        )(here, got, w_down)
    with jax.named_scope("swap_cores"):
        swapped = lax.ppermute(other, "core", [(0, 1), (1, 0)])
    with jax.named_scope("down_own"):
        tall = capacity + share
        own, right, left, far = pl.pallas_call(
            functools.partial(down_kernel, share),
            out_shape=[
                jax.ShapeDtypeStruct(shape, BF16)
                for shape in ((3, tall, LANE), (2, tall, LANE), (2, tall, LANE), (tall, LANE))
            ],
            in_specs=[SMEM, VMEM, VMEM, VMEM],
            out_specs=[VMEM] * 4,
            scratch_shapes=[pltpu.VMEM(half_shape.shape, BF16)],
            compiler_params=PARAMS,
            cost_estimate=cost(10**9, 4 * 10**6),
        )(here, rows, w_down, swapped)
    with jax.named_scope("sum_over_y"):
        def shifted(value, by):
            return lax.ppermute(value, "y", [(i, (i + by) % blocks) for i in range(blocks)])

        right, left, far = shifted(right, 1), shifted(left, -1), shifted(far, 2)
        right_two, left_two = pl.pallas_call(
            relay_kernel,
            out_shape=[jax.ShapeDtypeStruct((tall, LANE), BF16)] * 2,
            in_specs=[VMEM] * 4,
            out_specs=[VMEM] * 2,
            compiler_params=PARAMS,
            cost_estimate=cost(10**6, 2 * 10**6),
        )(own, right, left, far)
        right_two, left_two = shifted(right_two, 2), shifted(left_two, -2)
        scaled = pl.pallas_call(
            sum_kernel,
            out_shape=jax.ShapeDtypeStruct((capacity + share + 16, LANE), F32),
            in_specs=[VMEM] * 5,
            out_specs=VMEM,
            compiler_params=PARAMS,
            cost_estimate=cost(10**6, 3 * 10**6),
        )(own, right, left, right_two, left_two)
    with jax.named_scope("gather_hidden"):
        grad = lax.all_gather(scaled.astype(jnp.float16), ("y", "core"), axis=0).astype(F32)
    with jax.named_scope("back"):
        back = pl.pallas_call(
            functools.partial(back_kernel, share),
            out_shape=jax.ShapeDtypeStruct((packed, LANE), BF16),
            in_specs=[VMEM] * 8,
            out_specs=VMEM,
            scratch_shapes=[
                pltpu.VMEM((OWN, capacity, hidden), BF16),
                pltpu.VMEM((OWN, capacity, hidden), BF16),
                pltpu.VMEM((homes * MOST * 2 * OWN, LANE), BF16),
            ],
            compiler_params=PARAMS,
            cost_estimate=cost(2 * 10**9, 10**7),
        )(grad, rows, up_pre, up_factor, gate_factor, w_gate, w_up, select_out)
    with jax.named_scope("way_back"):
        home = lax.all_to_all(back.reshape(homes, PAIR, LANE), ("x", "z"), 0, 0, tiled=True).reshape(packed, LANE)
    with jax.named_scope("combine"):
        grad_tokens, grad_probs = pl.pallas_call(
            combine_kernel,
            out_shape=(
                jax.ShapeDtypeStruct((width, tokens), F32),
                jax.ShapeDtypeStruct(probs.shape[::-1], F32),
            ),
            in_specs=[VMEM] * 4,
            out_specs=(VMEM, VMEM),
            scratch_shapes=[pltpu.VMEM((2 * tokens, packed), BF16)],
            compiler_params=PARAMS,
            cost_estimate=cost(10**9, 10**6),
        )(routes.T, masks, pick, home)
        return grad_tokens.T, grad_probs.T


def solution(mesh):
    node, local = ("y", "core"), ("x", "z")
    y, x = mesh.devices.shape[0] // 2, 4
    parts = Mesh(mesh.devices.reshape(y, 2, x, -1), node + local)
    return jax.shard_map(
        on_device,
        mesh=parts,
        in_specs=(
            P(local, node),
            P(local, None),
            P(local, None),
            P(local, None, None),
            P(local, None, None),
            P(local, node, None),
            P(local, node, None),
            P(local, node, None),
        ),
        out_specs=(P(local, node), P(local, None)),
        check_vma=False,
    )
```
